32 devices in a mesh: section: 8 (over z, x), fsdp: 4 (over y, core).
Axes of the slice: x: 2, y: 2, z: 4, core: 2. Of those that a mesh axis runs over, the one named last changes fastest.
Arguments:
- acts: bfloat16 [8, 2304, 2048], P('section', 'fsdp'), may hold values from -6 to 6
- gains: float32 [8, 2048], P('section'), may hold values from 0.5 to 1.5
- proj: bfloat16 [8, 2048, 2048], P('section', 'fsdp'), may hold values from -0.0625 to 0.0625
- head: bfloat16 [2048, 512], replicated, may hold values from -1 to 1
- segs: int32 [12, 192], P('fsdp'), may hold values from 0 to 15, never falling along the last dimension, each value on 1 to 24 neighbouring positions
- labels: int32 [12, 16], P('fsdp'), may hold values from 0 to 511
Outputs:
- din: bfloat16 [8, 2304, 2048], P('section', 'fsdp')
- dproj: bfloat16 [8, 2048, 2048], P('section', 'fsdp')
- dgain: float32 [8, 2048], P('section')
The draws below stay inside these ranges and needn't reach their ends.
Inputs may be any that keep to these rules, and one draw needn't show every extreme that they name: `segs`: each row lists the candidates of one microbatch in order, every candidate has at least one token and one has 24.
All inputs are finite; a program needn't handle non-finite values.
Results may differ from the reference program's by a relative error of at most 0.04.
Values may be sent and summed in bfloat16 or wider, within the bound.
A program may use at most 128 MiB of HBM per device.

```python
import math
import jax
import jax.numpy as jnp
import numpy as np
from jax import lax

D = 2048
NCLS = 512
ROWS = 192
MOST = 24
CAND = 16
MBALL = 12
TOKENS = 2304
SECTIONS = 8


def touch_ends(result, own_key, least, high):
    longest = result.shape.index(max(result.shape))
    spots = []
    for shift in (0, 1):
        where = [jax.random.randint(jax.random.fold_in(own_key, axis), (), 0, length) for axis, length in enumerate(result.shape)]
        where[longest] = (where[longest] + shift) % result.shape[longest]
        spots.append(tuple(where))
    return result.at[spots[0]].set(least).at[spots[1]].set(high)


def shard_levels(rng, dims, shards, least, high):
    loudness = 1.0
    for position, shards_of in shards:
        steps = jax.random.uniform(jax.random.fold_in(jax.random.fold_in(rng, 6), position), (shards_of,), jnp.float32, least / len(shards), high / len(shards))
        loudness = loudness * jnp.repeat(jnp.exp(steps), dims[position] // shards_of).reshape((-1,) + (1,) * (len(dims) - 1 - position))
    return loudness


def profile(amount, total, reach, skew):
    weights = [(1 << 20) // math.isqrt(rank ** skew) + 1 for rank in range(2, amount + 1)]
    rest, given = total - reach - (amount - 1), [1] * (amount - 1)
    while rest > 0:
        movable = [i for i in range(amount - 1) if given[i] < reach]
        mass, remaining = sum([weights[i] for i in movable]), rest
        for i in movable:
            addition = min(reach - given[i], max(1, remaining * weights[i] // mass), rest)
            given[i] = given[i] + addition
            rest = rest - addition
    return np.array([reach] + given)


def uneven(rng, amount, total, limit, skew):
    if amount == 2:
        one = jax.random.randint(rng, (), max(1, total - limit), min(limit, total - 1) + 1)
        return jnp.stack([one, total - one])
    sizes = jnp.asarray(profile(amount, total, limit, skew), jnp.int32)
    pairs = (amount - 1) // 2
    source_of, sink = sizes[1:1 + 2 * pairs:2], sizes[2:2 + 2 * pairs:2]
    room = jnp.minimum(source_of - 1, limit - sink)
    shifted = jax.random.randint(jax.random.fold_in(rng, 1), (pairs,), 0, 1 << 20) % (room + 1)
    sizes = sizes.at[1:1 + 2 * pairs:2].set(source_of - shifted).at[2:2 + 2 * pairs:2].set(sink + shifted)
    return sizes[jax.random.permutation(jax.random.fold_in(rng, 2), amount)]


def scatter_about(rng, extent, scale, limit, shards=(), held_as=jnp.bfloat16):
    entries = scale * jax.random.normal(rng, extent, jnp.float32)
    if shards:
        entries = entries * shard_levels(rng, extent, shards, -0.22, 0.18)
    return jnp.clip(entries, -limit, limit).astype(held_as)


def setup_inputs(seed: int = 0) -> dict:
    arg_keys = jax.random.split(jax.random.key(seed), 7)
    acts = scatter_about(arg_keys[0], (SECTIONS, TOKENS, D), 1.0, 6.0, ((0, 8), (1, 4)))
    gains = jnp.clip(1.0 + 0.1 * jax.random.normal(arg_keys[1], (SECTIONS, D), jnp.float32), 0.5, 1.5)
    proj = scatter_about(arg_keys[2], (SECTIONS, D, D), (4 * D) ** -0.5, 0.0625, ((0, 8), (1, 4)))
    head = scatter_about(arg_keys[3], (D, NCLS), (D // 64) ** -0.5, 1.0)
    segs = jax.vmap(lambda own: jnp.searchsorted(jnp.cumsum(uneven(own, CAND, ROWS, MOST, 1)), jnp.arange(ROWS), side="right"))(jax.random.split(arg_keys[4], MBALL)).reshape((MBALL, ROWS)).astype(jnp.int32)
    labels = touch_ends(jax.random.randint(arg_keys[5], (MBALL, CAND), 0, NCLS), jax.random.fold_in(arg_keys[5], 1), 0, NCLS - 1).astype(jnp.int32)
    return {"acts": acts, "gains": gains, "proj": proj, "head": head, "segs": segs, "labels": labels}


norm_eps = 1e-06

def section_norm(layer_in, gain):
    x_float = layer_in.astype(jnp.float32)
    inv_rms = lax.rsqrt(lax.optimization_barrier(jnp.mean(x_float * x_float, -1, keepdims=True)) + norm_eps)
    x_hat = x_float * inv_rms
    return (x_hat, inv_rms, (x_hat * gain).astype(jnp.bfloat16))

def reference(acts, gains, proj, head, segs, labels):
    top = SECTIONS - 1
    x_hat, inv_rms, normed = section_norm(acts[top], gains[top])
    y_top = acts[top].astype(jnp.float32) + jnp.dot(normed, proj[top], preferred_element_type=jnp.float32)
    y_blocks = y_top.reshape(MBALL, ROWS, D)
    onehot = (segs[:, None, :] == jnp.arange(CAND, dtype=jnp.int32)[None, :, None]).astype(jnp.float32)
    counts = lax.optimization_barrier(jnp.sum(onehot, -1))
    pooled = (jnp.einsum('mcr,mrd->mcd', onehot, y_blocks) / counts[..., None]).astype(jnp.bfloat16)
    logits = jnp.dot(pooled.reshape(-1, D), head, preferred_element_type=jnp.float32)
    target = (labels.reshape(-1)[:, None] == jnp.arange(NCLS, dtype=jnp.int32)[None, :]).astype(jnp.float32)
    dlogit = (jax.nn.sigmoid(logits) - target).astype(jnp.bfloat16)
    dpool = jnp.dot(dlogit, head.T, preferred_element_type=jnp.float32).reshape(MBALL, CAND, D) / counts[..., None]
    grad = jnp.einsum('mcr,mcd->mrd', onehot, dpool).reshape(TOKENS, D).astype(jnp.bfloat16)
    din_list, dproj_list, dgain_list = ([], [], [])
    for section in reversed(range(SECTIONS)):
        x_hat, inv_rms, normed = section_norm(acts[section], gains[section])
        back = lax.dot_general(grad, proj[section], (((1,), (1,)), ((), ())), preferred_element_type=jnp.float32)
        scaled = back * gains[section]
        through = inv_rms * (scaled - x_hat * lax.optimization_barrier(jnp.mean(scaled * x_hat, -1, keepdims=True)))
        layer_grad = (grad.astype(jnp.float32) + through).astype(jnp.bfloat16)
        dgain_list.append(lax.optimization_barrier(jnp.sum(back * x_hat, 0)))
        weight_grad = lax.dot_general(normed, grad, (((0,), (0,)), ((), ())), preferred_element_type=jnp.float32)
        dproj_list.append(weight_grad.astype(jnp.bfloat16))
        din_list.append(layer_grad)
        grad = layer_grad
    din = jnp.stack(din_list[::-1])
    dproj = jnp.stack(dproj_list[::-1])
    dgain = jnp.stack(dgain_list[::-1])
    return (din, dproj, dgain)
```

```python
import functools

import jax
import jax.numpy as jnp
from jax import lax
from jax.experimental import pallas as pl
from jax.experimental.pallas import tpu as pltpu
from jax.sharding import PartitionSpec as P

norm_eps = 1e-06
MESH = pl.DeviceIdType.MESH
CHUNK = 64
PIECES = 4
bf16, f32 = jnp.bfloat16, jnp.float32
NT = (((1,), (1,)), ((), ()))
TN = (((0,), (0,)), ((), ()))


def kernel(
    sections, shards, chunks,
    acts, gain, wt_shard, head, pool, unpool, counts, labels,
    din, dproj, dgain,
    weight, grads, normed_own, normed_all, inv_rms, back_s, total, gain_acc, gain_all, top_g,
    local_sem, w_send, w_recv, n_send, n_recv, c_send, c_recv, g_send, g_recv, d_send, d_recv,
):
    sec = lax.axis_index("section")
    me = lax.axis_index("fsdp")
    top = sections - 1
    chips = shards // 2
    chip, core = me // 2, lax.rem(me, 2)
    pair = chip * 2 + 1 - core
    width = gain.shape[1]
    blk = width // shards
    rows = CHUNK
    is_top = sec == top

    def ahead(d):
        return lax.rem(chip + d, chips) * 2 + core

    def behind(d, own_core=True):
        return lax.rem(chip + chips - d, chips) * 2 + (core if own_core else 1 - core)

    barrier = pltpu.get_barrier_semaphore()
    for d in range(1, shards):
        pl.semaphore_signal(barrier, 1, device_id=(sec, lax.rem(me + d, shards)), device_id_type=MESH)

    @pl.when(sec > 0)
    def _():
        pl.semaphore_signal(barrier, 1, device_id=(sec - 1, me), device_id_type=MESH)

    @pl.when(sec < top)
    def _():
        pl.semaphore_signal(barrier, 1, device_id=(sec + 1, me), device_id_type=MESH)

    pl.semaphore_wait(
        barrier, shards - 1 + jnp.where(sec > 0, 1, 0) + jnp.where(sec < top, 1, 0)
    )

    def remote(src, dst, send, recv, dev):
        return pltpu.make_async_remote_copy(
            src_ref=src, dst_ref=dst, send_sem=send, recv_sem=recv,
            device_id=dev, device_id_type=MESH,
        )

    piece = width // PIECES

    def w_copy(p, kind, d, src_slot, target, own=False):
        span = pl.ds(p * piece, piece)
        n = 0 if kind == 0 else (d if kind == 1 else chips - 1 + d)
        src = wt_shard.at[span] if own else weight.at[src_slot, span]
        return remote(src, weight.at[src_slot, span], w_send.at[p, n], w_recv.at[p, n], (sec, target))

    own_w = pltpu.make_async_copy(wt_shard, weight.at[me], local_sem)
    own_w.start()
    for p in range(PIECES):
        for d in range(1, chips):
            w_copy(p, 1, d, me, ahead(d), own=True).start()
    for p in range(PIECES):
        w_copy(p, 0, 0, me, pair, own=True).start()

    def prep(k, carry):
        x = acts[k].astype(f32)
        inv = lax.rsqrt(jnp.mean(x * x, -1, keepdims=True) + norm_eps)
        inv_rms[k] = inv
        for b in range(shards):
            cols = slice(b * blk, (b + 1) * blk)
            normed_own[b, k] = (acts[k, :, cols].astype(f32) * inv * gain[:, cols]).astype(bf16)
        normed_all[k, me] = normed_own[me, k]
        return carry

    lax.fori_loop(0, chunks, prep, 0)
    gain_acc[...] = jnp.zeros_like(gain_acc)
    total[...] = jnp.zeros_like(total)

    for p in range(PIECES):
        for d in range(1, chips):
            w_copy(p, 1, d, behind(d), ahead(d)).wait_recv()
            w_copy(p, 2, d, behind(d), pair).start()
    for p in range(PIECES):
        w_copy(p, 0, 0, pair, pair).wait_recv()
        for d in range(1, chips):
            w_copy(p, 2, d, behind(d, False), pair).wait_recv()
    own_w.wait()

    def n_copy(d, src_slot, dst_slot):
        return remote(
            normed_own.at[src_slot], normed_all.at[:, dst_slot],
            n_send.at[d - 1], n_recv.at[d - 1], (sec, lax.rem(me + d, shards)),
        )

    for d in range(1, shards):
        n_copy(d, lax.rem(me + d, shards), me).start()

    @pl.when(is_top)
    def _():
        logits = 0.0
        sum_hi = []
        for b in range(shards):
            cols = slice(b * blk, (b + 1) * blk)
            pn = jnp.zeros((counts.shape[0], blk), f32)
            for k in range(chunks):
                pn = pn + jnp.dot(pool[k], normed_own[b, k], preferred_element_type=f32)
            hi = pn.astype(bf16)
            sum_hi.append(jnp.concatenate([hi, (pn - hi.astype(f32)).astype(bf16)], 0))
        for b in range(shards):
            cols = slice(b * blk, (b + 1) * blk)
            y = jnp.zeros((2 * counts.shape[0], blk), f32)
            for c in range(shards):
                y = y + lax.dot_general(
                    sum_hi[c], weight[c, cols, :], NT, preferred_element_type=f32
                )
            pooled = y[: counts.shape[0]] + y[counts.shape[0] :]
            for k in range(chunks):
                pooled = pooled + jnp.dot(pool[k], acts[k, :, cols], preferred_element_type=f32)
            pooled = (pooled / counts[...]).astype(bf16)
            logits = logits + jnp.dot(pooled, head[cols, :], preferred_element_type=f32)
        classes = lax.broadcasted_iota(jnp.int32, logits.shape, 1)
        target = jnp.where(classes == labels[...], 1.0, 0.0)
        dlogit = (jax.nn.sigmoid(logits) - target).astype(bf16)
        for b in range(shards):
            cols = slice(b * blk, (b + 1) * blk)
            dpool = lax.dot_general(dlogit, head[cols, :], NT, preferred_element_type=f32)
            top_g[:, cols] = (dpool / counts[...]).astype(bf16)

    def c_copy(k):
        return remote(din.at[k], grads.at[k, me], c_send.at[k], c_recv.at[k], (sec - 1, me))

    def g_copy(k, kind, d, slot, target):
        n = 0 if kind == 0 else (d if kind == 1 else chips - 1 + d)
        return remote(
            grads.at[k, slot], grads.at[k, slot], g_send.at[k, n], g_recv.at[k, n], (sec, target)
        )

    def relay(k):
        for d in range(1, chips):
            g_copy(k, 1, d, behind(d), ahead(d)).wait_recv()
            g_copy(k, 2, d, behind(d), pair).start()

    def accumulate(k):
        g_copy(k, 0, 0, pair, pair).wait_recv()
        for d in range(1, chips):
            g_copy(k, 2, d, behind(d, False), pair).wait_recv()
        lhs = normed_all[k].reshape(shards * rows, blk)
        for b in range(4):
            cols = slice(b * (width // 4), (b + 1) * (width // 4))
            rhs = grads[k, :, :, cols].reshape(shards * rows, width // 4)
            total[:, cols] += lax.dot_general(lhs, rhs, TN, preferred_element_type=f32)

    def step(k, carry):
        @pl.when(is_top)
        def _():
            grads[k, me] = jnp.dot(unpool[k], top_g[...], preferred_element_type=f32).astype(bf16)

        @pl.when(sec < top)
        def _():
            c_copy(k).wait_recv()

        g_copy(k, 0, 0, me, pair).start()
        for d in range(1, chips):
            g_copy(k, 1, d, me, ahead(d)).start()

        inv = inv_rms[k]
        dots = jnp.zeros((rows, 1), f32)
        for b in range(shards):
            cols = slice(b * blk, (b + 1) * blk)
            back = jnp.dot(grads[k, me], weight[b], preferred_element_type=f32)
            back_s[:, cols] = back
            prod = back * (acts[k, :, cols].astype(f32) * inv)
            gain_acc[:, cols] += jnp.sum(prod, 0, keepdims=True)
            dots = dots + jnp.sum(prod * gain[:, cols], -1, keepdims=True)
        mean = dots / width
        for b in range(shards):
            cols = slice(b * blk, (b + 1) * blk)
            x_hat = acts[k, :, cols].astype(f32) * inv
            through = inv * (back_s[:, cols] * gain[:, cols] - x_hat * mean)
            din[k, :, cols] = (grads[k, me, :, cols].astype(f32) + through).astype(bf16)

        @pl.when(sec > 0)
        def _():
            c_copy(k).start()

        @pl.when(jnp.logical_and(sec < top, k >= 1))
        def _():
            relay(k - 1)

        @pl.when(jnp.logical_and(sec < top, k == 2))
        def _():
            for d in range(1, shards):
                n_copy(d, me, lax.rem(me + shards - d, shards)).wait_recv()

        @pl.when(jnp.logical_and(sec < top, k >= 2))
        def _():
            accumulate(k - 2)

        return carry

    lax.fori_loop(0, chunks, step, 0)

    def d_copy(d, slot):
        return remote(
            gain_acc, gain_all.at[slot], d_send.at[d - 1], d_recv.at[d - 1],
            (sec, lax.rem(me + d, shards)),
        )

    for d in range(1, shards):
        d_copy(d, me).start()

    def relay_step(k, carry):
        relay(k)
        return carry

    def accumulate_step(k, carry):
        accumulate(k)
        return carry

    @pl.when(is_top)
    def _():
        for d in range(1, shards):
            n_copy(d, me, lax.rem(me + shards - d, shards)).wait_recv()
        lax.fori_loop(0, chunks - 1, relay_step, 0)
        lax.fori_loop(0, chunks - 2, accumulate_step, 0)

    relay(chunks - 1)
    lax.fori_loop(chunks - 2, chunks, accumulate_step, 0)
    dproj[...] = total[...].astype(bf16)

    gain_all[me] = gain_acc[...]
    for d in range(1, shards):
        d_copy(d, lax.rem(me + shards - d, shards)).wait_recv()
    dgain[...] = jnp.sum(gain_all[...], 0)

    for p in range(PIECES):
        w_copy(p, 0, 0, me, pair, own=True).wait_send()
        for d in range(1, chips):
            w_copy(p, 1, d, me, ahead(d), own=True).wait_send()
            w_copy(p, 2, d, behind(d), pair).wait_send()
    for d in range(1, shards):
        n_copy(d, lax.rem(me + d, shards), me).wait_send()
        d_copy(d, me).wait_send()

    def sent(k, carry):
        @pl.when(sec > 0)
        def _():
            c_copy(k).wait_send()

        g_copy(k, 0, 0, me, pair).wait_send()
        for d in range(1, chips):
            g_copy(k, 1, d, me, ahead(d)).wait_send()
            g_copy(k, 2, d, behind(d), pair).wait_send()
        return carry

    lax.fori_loop(0, chunks, sent, 0)


def per_device(sections, shards, acts, gains, proj, head, segs, labels):
    tokens, width = acts.shape[1:]
    batches, rows = segs.shape
    cands = labels.shape[1]
    classes = head.shape[1]
    blk = proj.shape[1]
    chunks = tokens // CHUNK
    chips = shards // 2
    every = batches * cands
    own = segs.reshape(-1) + cands * (jnp.arange(tokens, dtype=jnp.int32) // rows)
    hit = own[:, None] == jnp.arange(every, dtype=jnp.int32)[None, :]
    counts = jnp.sum(hit.astype(f32), 0)[:, None]
    unpool = hit.astype(bf16).reshape(chunks, CHUNK, every)
    pool = unpool.transpose(0, 2, 1)
    vmem = pl.BlockSpec(memory_space=pltpu.VMEM)
    dma = pltpu.SemaphoreType.DMA
    din, dproj, dgain = pl.pallas_call(
        functools.partial(kernel, sections, shards, chunks),
        out_shape=(
            jax.ShapeDtypeStruct((chunks, CHUNK, width), bf16),
            jax.ShapeDtypeStruct((blk, width), bf16),
            jax.ShapeDtypeStruct((1, width), f32),
        ),
        in_specs=[vmem, vmem, pl.BlockSpec(memory_space=pl.ANY)] + [vmem] * 5,
        out_specs=(vmem, vmem, vmem),
        scratch_shapes=[
            pltpu.VMEM((shards, width, blk), bf16),
            pltpu.VMEM((chunks, shards, CHUNK, width), bf16),
            pltpu.VMEM((shards, chunks, CHUNK, blk), bf16),
            pltpu.VMEM((chunks, shards, CHUNK, blk), bf16),
            pltpu.VMEM((chunks, CHUNK, 1), f32),
            pltpu.VMEM((CHUNK, width), f32),
            pltpu.VMEM((blk, width), f32),
            pltpu.VMEM((1, width), f32),
            pltpu.VMEM((shards, 1, width), f32),
            pltpu.VMEM((every, width), bf16),
            dma,
            dma((PIECES, 2 * chips - 1)),
            dma((PIECES, 2 * chips - 1)),
            dma((shards - 1,)),
            dma((shards - 1,)),
            dma((chunks,)),
            dma((chunks,)),
            dma((chunks, 2 * chips - 1)),
            dma((chunks, 2 * chips - 1)),
            dma((shards - 1,)),
            dma((shards - 1,)),
        ],
        compiler_params=pltpu.CompilerParams(
            collective_id=0, has_side_effects=True, vmem_limit_bytes=63 * 1024 * 1024
        ),
        cost_estimate=pl.CostEstimate(
            flops=4 * tokens * width * width, bytes_accessed=16 * width * width, transcendentals=0
        ),
    )(
        acts[0].reshape(chunks, CHUNK, width),
        gains,
        proj[0].T,
        head,
        pool,
        unpool,
        counts,
        labels.reshape(-1, 1),
    )
    return din.reshape(1, tokens, width), dproj[None], dgain


def solution(mesh):
    return jax.shard_map(
        functools.partial(per_device, mesh.shape["section"], mesh.shape["fsdp"]),
        mesh=mesh,
        in_specs=(
            P("section", "fsdp", None),
            P("section", None),
            P("section", "fsdp", None),
            P(),
            P("fsdp", None),
            P("fsdp", None),
        ),
        out_specs=(P("section", "fsdp", None), P("section", "fsdp", None), P("section", None)),
        check_vma=False,
    )
```

```python
import functools

import jax
import jax.numpy as jnp
from jax import lax
from jax.experimental import pallas as pl
from jax.experimental.pallas import tpu as pltpu
from jax.sharding import PartitionSpec as P

norm_eps = 1e-06
MESH = pl.DeviceIdType.MESH
CHUNK = 64
PIECES = 4
bf16, f32 = jnp.bfloat16, jnp.float32
NT = (((1,), (1,)), ((), ()))
TN = (((0,), (0,)), ((), ()))


def kernel(
    sections, shards, chunks,
    acts_hbm, gain, wt_shard, head_hbm, segs, labels,
    din, dproj, dgain,
    acts, head, weight, grads, normed_own, normed_all, inv_rms, back_s, total, gain_acc, gain_all,
    pool, part_out, part_in,
    local_sem, w_send, w_recv, n_send, n_recv, c_send, c_recv, g_send, g_recv, d_send, d_recv,
    t_send, t_recv,
):
    sec = lax.axis_index("section")
    me = lax.axis_index("fsdp")
    top = sections - 1
    chips = shards // 2
    chip, core = me // 2, lax.rem(me, 2)
    pair = chip * 2 + 1 - core
    width = gain.shape[1]
    blk = width // shards
    rows = CHUNK
    is_top = sec == top

    def ahead(d):
        return lax.rem(chip + d, chips) * 2 + core

    def behind(d, own_core=True):
        return lax.rem(chip + chips - d, chips) * 2 + (core if own_core else 1 - core)

    own_acts = pltpu.make_async_copy(acts_hbm, acts, local_sem.at[1])
    own_acts.start()
    own_w = pltpu.make_async_copy(wt_shard, weight.at[me], local_sem.at[0])
    own_w.start()
    own_head = pltpu.make_async_copy(head_hbm, head, local_sem.at[2])

    @pl.when(is_top)
    def _():
        own_head.start()

    barrier = pltpu.get_barrier_semaphore()
    for d in range(1, shards):
        pl.semaphore_signal(barrier, 1, device_id=(sec, lax.rem(me + d, shards)), device_id_type=MESH)

    @pl.when(sec > 0)
    def _():
        pl.semaphore_signal(barrier, 1, device_id=(sec - 1, me), device_id_type=MESH)

    @pl.when(sec < top)
    def _():
        pl.semaphore_signal(barrier, 1, device_id=(sec + 1, me), device_id_type=MESH)

    pl.semaphore_wait(
        barrier, shards - 1 + jnp.where(sec > 0, 1, 0) + jnp.where(sec < top, 1, 0)
    )

    def remote(src, dst, send, recv, dev):
        return pltpu.make_async_remote_copy(
            src_ref=src, dst_ref=dst, send_sem=send, recv_sem=recv,
            device_id=dev, device_id_type=MESH,
        )

    piece = width // PIECES

    def w_copy(p, kind, d, src_slot, target, own=False):
        span = pl.ds(p * piece, piece)
        n = 0 if kind == 0 else (d if kind == 1 else chips - 1 + d)
        src = wt_shard.at[span] if own else weight.at[src_slot, span]
        return remote(src, weight.at[src_slot, span], w_send.at[p, n], w_recv.at[p, n], (sec, target))

    @pl.when(sec < top)
    def _():
        for p in range(PIECES):
            for d in range(1, chips):
                w_copy(p, 1, d, me, ahead(d), own=True).start()
        for p in range(PIECES):
            w_copy(p, 0, 0, me, pair, own=True).start()

    own_acts.wait()

    def prep(k, carry):
        x = acts[k].astype(f32)
        inv = lax.rsqrt(jnp.mean(x * x, -1, keepdims=True) + norm_eps)
        inv_rms[k] = inv
        for b in range(shards):
            cols = slice(b * blk, (b + 1) * blk)
            normed_own[b, k] = (acts[k, :, cols].astype(f32) * inv * gain[:, cols]).astype(bf16)
        @pl.when(sec < top)
        def _():
            normed_all[k, me] = normed_own[me, k]

        return carry

    lax.fori_loop(0, chunks, prep, 0)
    gain_acc[...] = jnp.zeros_like(gain_acc)
    total[...] = jnp.zeros_like(total)

    own_w.wait()

    def n_copy(d, src_slot, dst_slot):
        return remote(
            normed_own.at[src_slot], normed_all.at[:, dst_slot],
            n_send.at[d - 1], n_recv.at[d - 1], (sec, lax.rem(me + d, shards)),
        )

    @pl.when(sec < top)
    def _():
        for p in range(PIECES):
            for d in range(1, chips):
                w_copy(p, 1, d, behind(d), ahead(d)).wait_recv()
                w_copy(p, 2, d, behind(d), pair).start()
        for p in range(PIECES):
            w_copy(p, 0, 0, pair, pair).wait_recv()
            for d in range(1, chips):
                w_copy(p, 2, d, behind(d, False), pair).wait_recv()
        for d in range(1, shards):
            n_copy(d, lax.rem(me + d, shards), me).start()

    batches, cands = labels.shape
    every = batches * cands
    per_batch = segs.shape[1] // rows
    classes = head.shape[1]
    quarter = width // 4

    def t_copy(n, src, dst, d):
        return remote(
            src, dst, t_send.at[n, d - 1], t_recv.at[n, d - 1], (sec, lax.rem(me + d, shards))
        )

    def sums_out(d):
        return t_copy(0, normed_all.at[0:2, lax.rem(me + d, shards), 0:every],
                      normed_all.at[2:4, me, 0:every], d)

    def parts_out(d):
        return t_copy(1, part_out.at[lax.rem(me + d, shards), :, 0:classes],
                      part_in.at[me, :, 0:classes], d)

    def grad_out(d):
        mine = grads.at[0, me, 0:every]
        return t_copy(2, mine, mine, d)

    def backs_out(d):
        return t_copy(3, part_out.at[lax.rem(me + d, shards), :, 0:blk],
                      part_in.at[me, :, 0:blk], d)

    def split(value):
        hi = value.astype(bf16)
        return hi, (value - hi.astype(f32)).astype(bf16)

    def flat(ref_value):
        return ref_value.reshape(shards * every, ref_value.shape[-1])

    @pl.when(is_top)
    def _():
        slots = lax.broadcasted_iota(jnp.int32, (every, rows), 0)
        counts = jnp.zeros((every, 1), f32)
        for k in range(chunks):
            m, at = k // per_batch, (k % per_batch) * rows
            hit = jnp.where(segs[m : m + 1, at : at + rows] + cands * m == slots, 1.0, 0.0)
            counts = counts + jnp.sum(hit, -1, keepdims=True)
            pool[k] = hit.astype(bf16)
        for b in range(shards):
            sums = jnp.zeros((every, blk), f32)
            for k in range(chunks):
                sums = sums + jnp.dot(pool[k], normed_own[b, k], preferred_element_type=f32)
            hi, lo = split(sums)
            normed_all[0, b, 0:every] = hi
            normed_all[1, b, 0:every] = lo
        for d in range(1, shards):
            sums_out(d).start()
        normed_all[2, me, 0:every] = normed_all[0, me, 0:every]
        normed_all[3, me, 0:every] = normed_all[1, me, 0:every]
        own_head.wait()
        logits = jnp.zeros((2 * every, classes), f32)
        for b in range(4):
            cols = slice(b * quarter, (b + 1) * quarter)
            sums = jnp.zeros((every, quarter), f32)
            for k in range(chunks):
                sums = sums + jnp.dot(pool[k], acts[k, :, cols], preferred_element_type=f32)
            logits = logits + jnp.dot(
                jnp.concatenate(split(sums), 0), head[cols, :], preferred_element_type=f32
            )
        logits = logits[:every] + logits[every:]
        for d in range(1, shards):
            sums_out(d).wait_recv()
        both = jnp.concatenate([flat(normed_all[n, :, 0:every]) for n in (2, 3)], 0)
        part = jnp.zeros((shards * every, classes), f32)
        for b in range(4):
            cols = slice(b * quarter, (b + 1) * quarter)
            y = lax.dot_general(both, weight[me, cols, :], NT, preferred_element_type=f32)
            y = (y[: shards * every] + y[shards * every :]).astype(bf16)
            part = part + jnp.dot(y, head[cols, :], preferred_element_type=f32)
        part_out[:, :, 0:classes] = part.reshape(shards, every, classes)
        for d in range(1, shards):
            parts_out(d).start()
        part_in[me] = part_out[me]
        for d in range(1, shards):
            parts_out(d).wait_recv()
        logits = (logits + jnp.sum(part_in[:, :, 0:classes], 0)) / counts
        lanes = lax.broadcasted_iota(jnp.int32, (cands, cands), 1)
        diagonal = lanes == lax.broadcasted_iota(jnp.int32, (cands, cands), 0)
        target = []
        for m in range(batches):
            own = jnp.where(diagonal, labels[m : m + 1, :].astype(f32), 0.0)
            target.append(jnp.sum(own, -1, keepdims=True))
        target = jnp.concatenate(target, 0).astype(jnp.int32)
        target = lax.broadcasted_iota(jnp.int32, (every, classes), 1) == target
        dlogit = (jax.nn.sigmoid(logits) - jnp.where(target, 1.0, 0.0)).astype(bf16)
        for b in range(4):
            cols = slice(b * quarter, (b + 1) * quarter)
            dpool = lax.dot_general(dlogit, head[cols, :], NT, preferred_element_type=f32)
            grads[0, me, 0:every, cols] = (dpool / counts).astype(bf16)
        for d in range(1, shards):
            grad_out(d).start()
        for d in range(1, shards):
            grad_out(d).wait_recv()
        for d in range(1, shards):
            parts_out(d).wait_send()
        part_out[:, :, 0:blk] = jnp.dot(
            flat(grads[0, :, 0:every]), weight[me], preferred_element_type=f32
        ).reshape(shards, every, blk)
        for d in range(1, shards):
            backs_out(d).start()
        part_in[me] = part_out[me]
        for d in range(1, shards):
            backs_out(d).wait_recv()
        for b in range(shards):
            hi, lo = split(part_in[b, :, 0:blk])
            normed_all[4, b, 0:every] = hi
            normed_all[5, b, 0:every] = lo

    def c_copy(k):
        return remote(din.at[k], grads.at[k, me], c_send.at[k], c_recv.at[k], (sec - 1, me))

    def g_copy(k, kind, d, slot, target):
        n = 0 if kind == 0 else (d if kind == 1 else chips - 1 + d)
        return remote(
            grads.at[k, slot], grads.at[k, slot], g_send.at[k, n], g_recv.at[k, n], (sec, target)
        )

    def relay(k):
        for d in range(1, chips):
            g_copy(k, 1, d, behind(d), ahead(d)).wait_recv()
            g_copy(k, 2, d, behind(d), pair).start()

    def accumulate(k):
        g_copy(k, 0, 0, pair, pair).wait_recv()
        for d in range(1, chips):
            g_copy(k, 2, d, behind(d, False), pair).wait_recv()
        lhs = normed_all[k].reshape(shards * rows, blk)
        for b in range(4):
            cols = slice(b * (width // 4), (b + 1) * (width // 4))
            rhs = grads[k, :, :, cols].reshape(shards * rows, width // 4)
            total[:, cols] += lax.dot_general(lhs, rhs, TN, preferred_element_type=f32)

    def section_back(k, back_of, grad_of):
        inv = inv_rms[k]
        dots = jnp.zeros((rows, 1), f32)
        for b in range(shards):
            cols = slice(b * blk, (b + 1) * blk)
            back = back_of(b)
            back_s[:, cols] = back
            prod = back * (acts[k, :, cols].astype(f32) * inv)
            gain_acc[:, cols] += jnp.sum(prod, 0, keepdims=True)
            dots = dots + jnp.sum(prod * gain[:, cols], -1, keepdims=True)
        mean = dots / width
        for b in range(shards):
            cols = slice(b * blk, (b + 1) * blk)
            x_hat = acts[k, :, cols].astype(f32) * inv
            through = inv * (back_s[:, cols] * gain[:, cols] - x_hat * mean)
            din[k, :, cols] = (grad_of(cols) + through).astype(bf16)

        @pl.when(sec > 0)
        def _():
            c_copy(k).start()

    def top_step(k, carry):
        def pick(value):
            return lax.dot_general(pool[k], value, TN, preferred_element_type=f32)

        section_back(
            k,
            lambda b: pick(normed_all[4, b, 0:every]) + pick(normed_all[5, b, 0:every]),
            lambda cols: pick(grads[0, me, 0:every, cols]),
        )
        return carry

    def step(k, carry):
        c_copy(k).wait_recv()
        g_copy(k, 0, 0, me, pair).start()
        for d in range(1, chips):
            g_copy(k, 1, d, me, ahead(d)).start()
        section_back(
            k,
            lambda b: jnp.dot(grads[k, me], weight[b], preferred_element_type=f32),
            lambda cols: grads[k, me, :, cols].astype(f32),
        )

        @pl.when(k >= 1)
        def _():
            relay(k - 1)

        @pl.when(k == 2)
        def _():
            for d in range(1, shards):
                n_copy(d, me, lax.rem(me + shards - d, shards)).wait_recv()

        @pl.when(k >= 2)
        def _():
            accumulate(k - 2)

        return carry

    @pl.when(is_top)
    def _():
        lax.fori_loop(0, chunks, top_step, 0)

    @pl.when(sec < top)
    def _():
        lax.fori_loop(0, chunks, step, 0)

    def d_copy(d, slot):
        return remote(
            gain_acc, gain_all.at[slot], d_send.at[d - 1], d_recv.at[d - 1],
            (sec, lax.rem(me + d, shards)),
        )

    for d in range(1, shards):
        d_copy(d, me).start()

    @pl.when(is_top)
    def _():
        every_grad = flat(grads[0, :, 0:every])
        for n in (2, 3):
            sums = flat(normed_all[n, :, 0:every])
            for b in range(4):
                cols = slice(b * quarter, (b + 1) * quarter)
                total[:, cols] += lax.dot_general(
                    sums, every_grad[:, cols], TN, preferred_element_type=f32
                )

    def accumulate_step(k, carry):
        accumulate(k)
        return carry

    @pl.when(sec < top)
    def _():
        relay(chunks - 1)
        lax.fori_loop(chunks - 2, chunks, accumulate_step, 0)

    dproj[...] = total[...].astype(bf16)

    gain_all[me] = gain_acc[...]
    for d in range(1, shards):
        d_copy(d, lax.rem(me + shards - d, shards)).wait_recv()
    dgain[...] = jnp.sum(gain_all[...], 0)

    for d in range(1, shards):
        d_copy(d, me).wait_send()

    @pl.when(is_top)
    def _():
        for d in range(1, shards):
            sums_out(d).wait_send()
            grad_out(d).wait_send()
            backs_out(d).wait_send()

    @pl.when(sec < top)
    def _():
        for p in range(PIECES):
            w_copy(p, 0, 0, me, pair, own=True).wait_send()
            for d in range(1, chips):
                w_copy(p, 1, d, me, ahead(d), own=True).wait_send()
                w_copy(p, 2, d, behind(d), pair).wait_send()
        for d in range(1, shards):
            n_copy(d, lax.rem(me + d, shards), me).wait_send()

    def sent(k, carry):
        @pl.when(sec > 0)
        def _():
            c_copy(k).wait_send()

        @pl.when(sec < top)
        def _():
            g_copy(k, 0, 0, me, pair).wait_send()
            for d in range(1, chips):
                g_copy(k, 1, d, me, ahead(d)).wait_send()
                g_copy(k, 2, d, behind(d), pair).wait_send()

        return carry

    lax.fori_loop(0, chunks, sent, 0)


def per_device(sections, shards, acts, gains, proj, head, segs, labels):
    tokens, width = acts.shape[1:]
    batches, rows = segs.shape
    cands = labels.shape[1]
    classes = head.shape[1]
    blk = proj.shape[1]
    chunks = tokens // CHUNK
    chips = shards // 2
    every = batches * cands
    vmem = pl.BlockSpec(memory_space=pltpu.VMEM)
    hbm = pl.BlockSpec(memory_space=pl.ANY)
    dma = pltpu.SemaphoreType.DMA
    din, dproj, dgain = pl.pallas_call(
        functools.partial(kernel, sections, shards, chunks),
        out_shape=(
            jax.ShapeDtypeStruct((chunks, CHUNK, width), bf16),
            jax.ShapeDtypeStruct((blk, width), bf16),
            jax.ShapeDtypeStruct((1, width), f32),
        ),
        in_specs=[hbm, vmem, hbm, hbm, vmem, vmem],
        out_specs=(vmem, vmem, vmem),
        scratch_shapes=[
            pltpu.VMEM((chunks, CHUNK, width), bf16),
            pltpu.VMEM((width, classes), bf16),
            pltpu.VMEM((shards, width, blk), bf16),
            pltpu.VMEM((chunks, shards, CHUNK, width), bf16),
            pltpu.VMEM((shards, chunks, CHUNK, blk), bf16),
            pltpu.VMEM((chunks, shards, CHUNK, blk), bf16),
            pltpu.VMEM((chunks, CHUNK, 1), f32),
            pltpu.VMEM((CHUNK, width), f32),
            pltpu.VMEM((blk, width), f32),
            pltpu.VMEM((1, width), f32),
            pltpu.VMEM((shards, 1, width), f32),
            pltpu.VMEM((chunks, every, CHUNK), bf16),
            pltpu.VMEM((shards, every, max(classes, blk)), f32),
            pltpu.VMEM((shards, every, max(classes, blk)), f32),
            dma((3,)),
            dma((PIECES, 2 * chips - 1)),
            dma((PIECES, 2 * chips - 1)),
            dma((shards - 1,)),
            dma((shards - 1,)),
            dma((chunks,)),
            dma((chunks,)),
            dma((chunks, 2 * chips - 1)),
            dma((chunks, 2 * chips - 1)),
            dma((shards - 1,)),
            dma((shards - 1,)),
            dma((4, shards - 1)),
            dma((4, shards - 1)),
        ],
        compiler_params=pltpu.CompilerParams(
            collective_id=0, has_side_effects=True, vmem_limit_bytes=127 * 512 * 1024
        ),
        cost_estimate=pl.CostEstimate(
            flops=4 * tokens * width * width, bytes_accessed=16 * width * width, transcendentals=0
        ),
    )(
        acts[0].reshape(chunks, CHUNK, width),
        gains,
        proj[0].T,
        head,
        segs,
        labels,
    )
    return din.reshape(1, tokens, width), dproj[None], dgain


def solution(mesh):
    return jax.shard_map(
        functools.partial(per_device, mesh.shape["section"], mesh.shape["fsdp"]),
        mesh=mesh,
        in_specs=(
            P("section", "fsdp", None),
            P("section", None),
            P("section", "fsdp", None),
            P(),
            P("fsdp", None),
            P("fsdp", None),
        ),
        out_specs=(P("section", "fsdp", None), P("section", "fsdp", None), P("section", None)),
        check_vma=False,
    )
```

```python
import functools

import jax
import jax.numpy as jnp
from jax import lax
from jax.experimental import pallas as pl
from jax.experimental.pallas import tpu as pltpu
from jax.sharding import PartitionSpec as P

norm_eps = 1e-06
MESH = pl.DeviceIdType.MESH
CHUNK = 64
PIECES = 16
LENT = 7
bf16, f32 = jnp.bfloat16, jnp.float32
NT = (((1,), (1,)), ((), ()))
TN = (((0,), (0,)), ((), ()))


def kernel(
    sections, shards, chunks,
    acts_hbm, gain, wt_shard, head_hbm, segs, labels,
    din, dproj, dgain,
    acts, head, weight, grads, normed_own, normed_all, inv_rms, back_s, total, gain_acc, gain_all,
    pool, part_out, part_in, via_in, via_out,
    local_sem, w_send, w_recv, n_send, n_recv, c_send, c_recv, g_send, g_recv, d_send, d_recv,
    t_send, t_recv, v_send, v_recv,
):
    sec = lax.axis_index("section")
    me = lax.axis_index("fsdp")
    top = sections - 1
    chips = shards // 2
    chip, core = me // 2, lax.rem(me, 2)
    pair = chip * 2 + 1 - core
    width = gain.shape[1]
    blk = width // shards
    rows = CHUNK
    is_top = sec == top
    lending = chips == 2 and sections >= 8
    other = top - 1 - sec
    borrows = jnp.logical_and(lending, jnp.logical_and(sec >= top - 2, sec < top))
    lends = jnp.logical_and(lending, sec <= 1)
    lone = jnp.logical_not(borrows)
    direct = list(range(PIECES - LENT))
    lent = list(range(PIECES - LENT, PIECES))
    order = [p for i in direct for p in (direct[i : i + 1] + lent[i : i + 1])]

    def ahead(d):
        return lax.rem(chip + d, chips) * 2 + core

    def behind(d, own_core=True):
        return lax.rem(chip + chips - d, chips) * 2 + (core if own_core else 1 - core)

    own_acts = pltpu.make_async_copy(acts_hbm, acts, local_sem.at[1])
    own_acts.start()
    own_w = pltpu.make_async_copy(wt_shard, weight.at[me], local_sem.at[0])
    own_w.start()
    own_head = pltpu.make_async_copy(head_hbm, head, local_sem.at[2])

    @pl.when(is_top)
    def _():
        own_head.start()

    barrier = pltpu.get_barrier_semaphore()
    for d in range(1, shards):
        pl.semaphore_signal(barrier, 1, device_id=(sec, lax.rem(me + d, shards)), device_id_type=MESH)

    @pl.when(sec > 0)
    def _():
        pl.semaphore_signal(barrier, 1, device_id=(sec - 1, me), device_id_type=MESH)

    @pl.when(sec < top)
    def _():
        pl.semaphore_signal(barrier, 1, device_id=(sec + 1, me), device_id_type=MESH)

    @pl.when(jnp.logical_or(borrows, lends))
    def _():
        pl.semaphore_signal(barrier, 1, device_id=(other, me), device_id_type=MESH)

    pl.semaphore_wait(
        barrier,
        shards - 1
        + jnp.where(sec > 0, 1, 0)
        + jnp.where(sec < top, 1, 0)
        + jnp.where(jnp.logical_or(borrows, lends), 1, 0),
    )

    def remote(src, dst, send, recv, dev):
        return pltpu.make_async_remote_copy(
            src_ref=src, dst_ref=dst, send_sem=send, recv_sem=recv,
            device_id=dev, device_id_type=MESH,
        )

    piece = width // PIECES

    def w_copy(p, kind, d, src_slot, target, own=False):
        span = pl.ds(p * piece, piece)
        n = 0 if kind == 0 else (d if kind == 1 else chips - 1 + d)
        src = wt_shard.at[span] if own else weight.at[src_slot, span]
        return remote(src, weight.at[src_slot, span], w_send.at[p, n], w_recv.at[p, n], (sec, target))

    def v_copy(hop, i):
        span = pl.ds((PIECES - LENT + i) * piece, piece)
        if hop == 0:
            src, dst, dev = wt_shard.at[span], via_in.at[i], (other, me)
        elif hop == 1:
            src, dst, dev = via_in.at[i], via_out.at[i], (sec, ahead(1))
        else:
            src, dst, dev = via_out.at[i], weight.at[ahead(1), span], (other, me)
        recv = w_recv.at[PIECES - LENT + i, 1] if hop == 2 else v_recv.at[hop, i]
        return remote(src, dst, v_send.at[hop, i], recv, dev)

    if lending:
        @pl.when(borrows)
        def _():
            for i in range(LENT):
                v_copy(0, i).start()

        @pl.when(lends)
        def _():
            for i in range(LENT + 1):
                if i < LENT:
                    v_copy(0, i).wait_recv()
                    v_copy(1, i).start()
                if i > 0:
                    v_copy(1, i - 1).wait_recv()
                    v_copy(2, i - 1).start()

    @pl.when(sec < top)
    def _():
        for p in direct:
            for d in range(1, chips):
                w_copy(p, 1, d, me, ahead(d), own=True).start()

        @pl.when(lone)
        def _():
            for p in lent:
                for d in range(1, chips):
                    w_copy(p, 1, d, me, ahead(d), own=True).start()

        for p in order:
            w_copy(p, 0, 0, me, pair, own=True).start()

    own_acts.wait()

    def prep(k, carry):
        x = acts[k].astype(f32)
        inv = lax.rsqrt(jnp.mean(x * x, -1, keepdims=True) + norm_eps)
        inv_rms[k] = inv
        for b in range(shards):
            cols = slice(b * blk, (b + 1) * blk)
            normed_own[b, k] = (acts[k, :, cols].astype(f32) * inv * gain[:, cols]).astype(bf16)
        @pl.when(sec < top)
        def _():
            normed_all[k, me] = normed_own[me, k]

        return carry

    lax.fori_loop(0, chunks, prep, 0)
    gain_acc[...] = jnp.zeros_like(gain_acc)
    total[...] = jnp.zeros_like(total)

    own_w.wait()

    def n_copy(d, src_slot, dst_slot):
        return remote(
            normed_own.at[src_slot], normed_all.at[:, dst_slot],
            n_send.at[d - 1], n_recv.at[d - 1], (sec, lax.rem(me + d, shards)),
        )

    @pl.when(sec < top)
    def _():
        for p in order:
            for d in range(1, chips):
                w_copy(p, 1, d, behind(d), ahead(d)).wait_recv()
                w_copy(p, 2, d, behind(d), pair).start()
        for p in range(PIECES):
            w_copy(p, 0, 0, pair, pair).wait_recv()
            for d in range(1, chips):
                w_copy(p, 2, d, behind(d, False), pair).wait_recv()
        for d in range(1, shards):
            n_copy(d, lax.rem(me + d, shards), me).start()

    batches, cands = labels.shape
    every = batches * cands
    per_batch = segs.shape[1] // rows
    classes = head.shape[1]
    quarter = width // 4

    def t_copy(n, src, dst, d):
        return remote(
            src, dst, t_send.at[n, d - 1], t_recv.at[n, d - 1], (sec, lax.rem(me + d, shards))
        )

    def sums_out(d):
        return t_copy(0, normed_all.at[0:2, lax.rem(me + d, shards), 0:every],
                      normed_all.at[2:4, me, 0:every], d)

    def parts_out(d):
        return t_copy(1, part_out.at[lax.rem(me + d, shards), :, 0:classes],
                      part_in.at[me, :, 0:classes], d)

    def grad_out(d):
        mine = grads.at[0, me, 0:every]
        return t_copy(2, mine, mine, d)

    def backs_out(d):
        return t_copy(3, part_out.at[lax.rem(me + d, shards), :, 0:blk],
                      part_in.at[me, :, 0:blk], d)

    def split(value):
        hi = value.astype(bf16)
        return hi, (value - hi.astype(f32)).astype(bf16)

    def flat(ref_value):
        return ref_value.reshape(shards * every, ref_value.shape[-1])

    @pl.when(is_top)
    def _():
        slots = lax.broadcasted_iota(jnp.int32, (every, rows), 0)
        counts = jnp.zeros((every, 1), f32)
        for k in range(chunks):
            m, at = k // per_batch, (k % per_batch) * rows
            hit = jnp.where(segs[m : m + 1, at : at + rows] + cands * m == slots, 1.0, 0.0)
            counts = counts + jnp.sum(hit, -1, keepdims=True)
            pool[k] = hit.astype(bf16)
        for b in range(shards):
            sums = jnp.zeros((every, blk), f32)
            for k in range(chunks):
                sums = sums + jnp.dot(pool[k], normed_own[b, k], preferred_element_type=f32)
            hi, lo = split(sums)
            normed_all[0, b, 0:every] = hi
            normed_all[1, b, 0:every] = lo
        for d in range(1, shards):
            sums_out(d).start()
        normed_all[2, me, 0:every] = normed_all[0, me, 0:every]
        normed_all[3, me, 0:every] = normed_all[1, me, 0:every]
        own_head.wait()
        logits = jnp.zeros((2 * every, classes), f32)
        for b in range(4):
            cols = slice(b * quarter, (b + 1) * quarter)
            sums = jnp.zeros((every, quarter), f32)
            for k in range(chunks):
                sums = sums + jnp.dot(pool[k], acts[k, :, cols], preferred_element_type=f32)
            logits = logits + jnp.dot(
                jnp.concatenate(split(sums), 0), head[cols, :], preferred_element_type=f32
            )
        logits = logits[:every] + logits[every:]
        for d in range(1, shards):
            sums_out(d).wait_recv()
        both = jnp.concatenate([flat(normed_all[n, :, 0:every]) for n in (2, 3)], 0)
        part = jnp.zeros((shards * every, classes), f32)
        for b in range(4):
            cols = slice(b * quarter, (b + 1) * quarter)
            y = lax.dot_general(both, weight[me, cols, :], NT, preferred_element_type=f32)
            y = (y[: shards * every] + y[shards * every :]).astype(bf16)
            part = part + jnp.dot(y, head[cols, :], preferred_element_type=f32)
        part_out[:, :, 0:classes] = part.reshape(shards, every, classes)
        for d in range(1, shards):
            parts_out(d).start()
        part_in[me] = part_out[me]
        for d in range(1, shards):
            parts_out(d).wait_recv()
        logits = (logits + jnp.sum(part_in[:, :, 0:classes], 0)) / counts
        lanes = lax.broadcasted_iota(jnp.int32, (cands, cands), 1)
        diagonal = lanes == lax.broadcasted_iota(jnp.int32, (cands, cands), 0)
        target = []
        for m in range(batches):
            own = jnp.where(diagonal, labels[m : m + 1, :].astype(f32), 0.0)
            target.append(jnp.sum(own, -1, keepdims=True))
        target = jnp.concatenate(target, 0).astype(jnp.int32)
        target = lax.broadcasted_iota(jnp.int32, (every, classes), 1) == target
        dlogit = (jax.nn.sigmoid(logits) - jnp.where(target, 1.0, 0.0)).astype(bf16)
        for b in range(4):
            cols = slice(b * quarter, (b + 1) * quarter)
            dpool = lax.dot_general(dlogit, head[cols, :], NT, preferred_element_type=f32)
            grads[0, me, 0:every, cols] = (dpool / counts).astype(bf16)
        for d in range(1, shards):
            grad_out(d).start()
        for d in range(1, shards):
            grad_out(d).wait_recv()
        for d in range(1, shards):
            parts_out(d).wait_send()
        part_out[:, :, 0:blk] = jnp.dot(
            flat(grads[0, :, 0:every]), weight[me], preferred_element_type=f32
        ).reshape(shards, every, blk)
        for d in range(1, shards):
            backs_out(d).start()
        part_in[me] = part_out[me]
        for d in range(1, shards):
            backs_out(d).wait_recv()
        for b in range(shards):
            hi, lo = split(part_in[b, :, 0:blk])
            normed_all[4, b, 0:every] = hi
            normed_all[5, b, 0:every] = lo

    def c_copy(k):
        return remote(din.at[k], grads.at[k, me], c_send.at[k], c_recv.at[k], (sec - 1, me))

    def g_copy(k, kind, d, slot, target):
        n = 0 if kind == 0 else (d if kind == 1 else chips - 1 + d)
        return remote(
            grads.at[k, slot], grads.at[k, slot], g_send.at[k, n], g_recv.at[k, n], (sec, target)
        )

    def relay(k):
        for d in range(1, chips):
            g_copy(k, 1, d, behind(d), ahead(d)).wait_recv()
            g_copy(k, 2, d, behind(d), pair).start()

    def accumulate(k):
        g_copy(k, 0, 0, pair, pair).wait_recv()
        for d in range(1, chips):
            g_copy(k, 2, d, behind(d, False), pair).wait_recv()
        lhs = normed_all[k].reshape(shards * rows, blk)
        for b in range(4):
            cols = slice(b * (width // 4), (b + 1) * (width // 4))
            rhs = grads[k, :, :, cols].reshape(shards * rows, width // 4)
            total[:, cols] += lax.dot_general(lhs, rhs, TN, preferred_element_type=f32)

    lag = jnp.clip(1 + 2 * (sec - (top - 4)), 1, chunks)

    def columns_here():
        for d in range(1, shards):
            n_copy(d, me, lax.rem(me + shards - d, shards)).wait_recv()

    def section_back(k, back_of, grad_of):
        inv = inv_rms[k]
        dots = jnp.zeros((rows, 1), f32)
        for b in range(shards):
            cols = slice(b * blk, (b + 1) * blk)
            back = back_of(b)
            back_s[:, cols] = back
            prod = back * (acts[k, :, cols].astype(f32) * inv)
            gain_acc[:, cols] += jnp.sum(prod, 0, keepdims=True)
            dots = dots + jnp.sum(prod * gain[:, cols], -1, keepdims=True)
        mean = dots / width
        for b in range(shards):
            cols = slice(b * blk, (b + 1) * blk)
            x_hat = acts[k, :, cols].astype(f32) * inv
            through = inv * (back_s[:, cols] * gain[:, cols] - x_hat * mean)
            din[k, :, cols] = (grad_of(cols) + through).astype(bf16)

        @pl.when(sec > 0)
        def _():
            c_copy(k).start()

    def top_step(k, carry):
        def pick(value):
            return lax.dot_general(pool[k], value, TN, preferred_element_type=f32)

        section_back(
            k,
            lambda b: pick(normed_all[4, b, 0:every]) + pick(normed_all[5, b, 0:every]),
            lambda cols: pick(grads[0, me, 0:every, cols]),
        )
        return carry

    def step(k, carry):
        c_copy(k).wait_recv()
        g_copy(k, 0, 0, me, pair).start()
        for d in range(1, chips):
            g_copy(k, 1, d, me, ahead(d)).start()
        section_back(
            k,
            lambda b: jnp.dot(grads[k, me], weight[b], preferred_element_type=f32),
            lambda cols: grads[k, me, :, cols].astype(f32),
        )

        @pl.when(k >= lag)
        def _():
            relay(k - lag)

        @pl.when(k == lag + 1)
        def _():
            columns_here()

        @pl.when(k >= lag + 1)
        def _():
            accumulate(k - lag - 1)

        return carry

    @pl.when(is_top)
    def _():
        lax.fori_loop(0, chunks, top_step, 0)

    @pl.when(sec < top)
    def _():
        lax.fori_loop(0, chunks, step, 0)

    def d_copy(d, slot):
        return remote(
            gain_acc, gain_all.at[slot], d_send.at[d - 1], d_recv.at[d - 1],
            (sec, lax.rem(me + d, shards)),
        )

    for d in range(1, shards):
        d_copy(d, me).start()

    @pl.when(is_top)
    def _():
        every_grad = flat(grads[0, :, 0:every])
        for n in (2, 3):
            sums = flat(normed_all[n, :, 0:every])
            for b in range(4):
                cols = slice(b * quarter, (b + 1) * quarter)
                total[:, cols] += lax.dot_general(
                    sums, every_grad[:, cols], TN, preferred_element_type=f32
                )

    def relay_step(k, carry):
        relay(k)
        return carry

    def accumulate_step(k, carry):
        accumulate(k)
        return carry

    @pl.when(sec < top)
    def _():
        @pl.when(lag + 1 >= chunks)
        def _():
            columns_here()

        lax.fori_loop(chunks - lag, chunks, relay_step, 0)
        lax.fori_loop(jnp.maximum(chunks - lag - 1, 0), chunks, accumulate_step, 0)

    dproj[...] = total[...].astype(bf16)

    gain_all[me] = gain_acc[...]
    for d in range(1, shards):
        d_copy(d, lax.rem(me + shards - d, shards)).wait_recv()
    dgain[...] = jnp.sum(gain_all[...], 0)

    for d in range(1, shards):
        d_copy(d, me).wait_send()

    @pl.when(is_top)
    def _():
        for d in range(1, shards):
            sums_out(d).wait_send()
            grad_out(d).wait_send()
            backs_out(d).wait_send()

    @pl.when(sec < top)
    def _():
        for p in range(PIECES):
            w_copy(p, 0, 0, me, pair, own=True).wait_send()
            for d in range(1, chips):
                w_copy(p, 2, d, behind(d), pair).wait_send()
        for p in direct:
            for d in range(1, chips):
                w_copy(p, 1, d, me, ahead(d), own=True).wait_send()

        @pl.when(lone)
        def _():
            for p in lent:
                for d in range(1, chips):
                    w_copy(p, 1, d, me, ahead(d), own=True).wait_send()

        for d in range(1, shards):
            n_copy(d, lax.rem(me + d, shards), me).wait_send()

    if lending:
        @pl.when(borrows)
        def _():
            for i in range(LENT):
                v_copy(0, i).wait_send()

        @pl.when(lends)
        def _():
            for i in range(LENT):
                v_copy(1, i).wait_send()
                v_copy(2, i).wait_send()

    def sent(k, carry):
        @pl.when(sec > 0)
        def _():
            c_copy(k).wait_send()

        @pl.when(sec < top)
        def _():
            g_copy(k, 0, 0, me, pair).wait_send()
            for d in range(1, chips):
                g_copy(k, 1, d, me, ahead(d)).wait_send()
                g_copy(k, 2, d, behind(d), pair).wait_send()

        return carry

    lax.fori_loop(0, chunks, sent, 0)


def per_device(sections, shards, acts, gains, proj, head, segs, labels):
    tokens, width = acts.shape[1:]
    batches, rows = segs.shape
    cands = labels.shape[1]
    classes = head.shape[1]
    blk = proj.shape[1]
    chunks = tokens // CHUNK
    chips = shards // 2
    every = batches * cands
    vmem = pl.BlockSpec(memory_space=pltpu.VMEM)
    hbm = pl.BlockSpec(memory_space=pl.ANY)
    dma = pltpu.SemaphoreType.DMA
    din, dproj, dgain = pl.pallas_call(
        functools.partial(kernel, sections, shards, chunks),
        out_shape=(
            jax.ShapeDtypeStruct((chunks, CHUNK, width), bf16),
            jax.ShapeDtypeStruct((blk, width), bf16),
            jax.ShapeDtypeStruct((1, width), f32),
        ),
        in_specs=[hbm, vmem, hbm, hbm, vmem, vmem],
        out_specs=(vmem, vmem, vmem),
        scratch_shapes=[
            pltpu.VMEM((chunks, CHUNK, width), bf16),
            pltpu.VMEM((width, classes), bf16),
            pltpu.VMEM((shards, width, blk), bf16),
            pltpu.VMEM((chunks, shards, CHUNK, width), bf16),
            pltpu.VMEM((shards, chunks, CHUNK, blk), bf16),
            pltpu.VMEM((chunks, shards, CHUNK, blk), bf16),
            pltpu.VMEM((chunks, CHUNK, 1), f32),
            pltpu.VMEM((CHUNK, width), f32),
            pltpu.VMEM((blk, width), f32),
            pltpu.VMEM((1, width), f32),
            pltpu.VMEM((shards, 1, width), f32),
            pltpu.VMEM((chunks, every, CHUNK), bf16),
            pltpu.VMEM((shards, every, max(classes, blk)), f32),
            pltpu.VMEM((shards, every, max(classes, blk)), f32),
            pltpu.VMEM((LENT, width // PIECES if chips == 2 else 16, blk), bf16),
            pltpu.VMEM((LENT, width // PIECES if chips == 2 else 16, blk), bf16),
            dma((3,)),
            dma((PIECES, 2 * chips - 1)),
            dma((PIECES, 2 * chips - 1)),
            dma((shards - 1,)),
            dma((shards - 1,)),
            dma((chunks,)),
            dma((chunks,)),
            dma((chunks, 2 * chips - 1)),
            dma((chunks, 2 * chips - 1)),
            dma((shards - 1,)),
            dma((shards - 1,)),
            dma((4, shards - 1)),
            dma((4, shards - 1)),
            dma((3, LENT)),
            dma((3, LENT)),
        ],
        compiler_params=pltpu.CompilerParams(
            collective_id=0, has_side_effects=True, vmem_limit_bytes=127 * 512 * 1024
        ),
        cost_estimate=pl.CostEstimate(
            flops=4 * tokens * width * width, bytes_accessed=16 * width * width, transcendentals=0
        ),
    )(
        acts[0].reshape(chunks, CHUNK, width),
        gains,
        proj[0].T,
        head,
        segs,
        labels,
    )
    return din.reshape(1, tokens, width), dproj[None], dgain


def solution(mesh):
    return jax.shard_map(
        functools.partial(per_device, mesh.shape["section"], mesh.shape["fsdp"]),
        mesh=mesh,
        in_specs=(
            P("section", "fsdp", None),
            P("section", None),
            P("section", "fsdp", None),
            P(),
            P("fsdp", None),
            P("fsdp", None),
        ),
        out_specs=(P("section", "fsdp", None), P("section", "fsdp", None), P("section", None)),
        check_vma=False,
    )
```

```python
import functools

import jax
import jax.numpy as jnp
from jax import lax
from jax.experimental import pallas as pl
from jax.experimental.pallas import tpu as pltpu
from jax.sharding import PartitionSpec as P

norm_eps = 1e-06
MESH = pl.DeviceIdType.MESH
CHUNK = 64
PIECES = 16
LENT = 5
bf16, f32 = jnp.bfloat16, jnp.float32
NT = (((1,), (1,)), ((), ()))
TN = (((0,), (0,)), ((), ()))


def kernel(
    sections, shards, chunks,
    acts_hbm, gain, wt_shard, head_hbm, segs, labels,
    din, dproj, dgain,
    acts, head, weight, grads, normed_own, normed_all, inv_rms, back_s, total, gain_acc, gain_all,
    pool, part_out, part_in, via_in, via_out,
    local_sem, w_send, w_recv, n_send, n_recv, c_send, c_recv, g_send, g_recv, d_send, d_recv,
    t_send, t_recv, v_send, v_recv,
):
    sec = lax.axis_index("section")
    me = lax.axis_index("fsdp")
    top = sections - 1
    chips = shards // 2
    chip, core = me // 2, lax.rem(me, 2)
    pair = chip * 2 + 1 - core
    width = gain.shape[1]
    blk = width // shards
    rows = CHUNK
    is_top = sec == top
    lending = chips == 2 and sections >= 8
    other = top - 1 - sec
    borrows = jnp.logical_and(lending, jnp.logical_and(sec >= top - 2, sec < top))
    lends = jnp.logical_and(lending, sec <= 1)
    lone = jnp.logical_not(borrows)
    direct = list(range(PIECES - LENT))
    lent = list(range(PIECES - LENT, PIECES))
    order = [p for i in direct for p in (direct[i : i + 1] + lent[i : i + 1])]

    def ahead(d):
        return lax.rem(chip + d, chips) * 2 + core

    def behind(d, own_core=True):
        return lax.rem(chip + chips - d, chips) * 2 + (core if own_core else 1 - core)

    own_acts = pltpu.make_async_copy(acts_hbm, acts, local_sem.at[1])
    own_acts.start()
    own_w = pltpu.make_async_copy(wt_shard, weight.at[me], local_sem.at[0])
    own_w.start()
    own_head = pltpu.make_async_copy(head_hbm, head, local_sem.at[2])

    @pl.when(is_top)
    def _():
        own_head.start()

    barrier = pltpu.get_barrier_semaphore()
    for d in range(1, shards):
        pl.semaphore_signal(barrier, 1, device_id=(sec, lax.rem(me + d, shards)), device_id_type=MESH)

    @pl.when(sec > 0)
    def _():
        pl.semaphore_signal(barrier, 1, device_id=(sec - 1, me), device_id_type=MESH)

    @pl.when(sec < top)
    def _():
        pl.semaphore_signal(barrier, 1, device_id=(sec + 1, me), device_id_type=MESH)

    @pl.when(jnp.logical_or(borrows, lends))
    def _():
        pl.semaphore_signal(barrier, 1, device_id=(other, me), device_id_type=MESH)

    pl.semaphore_wait(
        barrier,
        shards - 1
        + jnp.where(sec > 0, 1, 0)
        + jnp.where(sec < top, 1, 0)
        + jnp.where(jnp.logical_or(borrows, lends), 1, 0),
    )

    def remote(src, dst, send, recv, dev):
        return pltpu.make_async_remote_copy(
            src_ref=src, dst_ref=dst, send_sem=send, recv_sem=recv,
            device_id=dev, device_id_type=MESH,
        )

    piece = width // PIECES

    def w_copy(p, kind, d, src_slot, target, own=False):
        span = pl.ds(p * piece, piece)
        n = 0 if kind == 0 else (d if kind == 1 else chips - 1 + d)
        src = wt_shard.at[span] if own else weight.at[src_slot, span]
        return remote(src, weight.at[src_slot, span], w_send.at[p, n], w_recv.at[p, n], (sec, target))

    def v_copy(hop, i):
        span = pl.ds((PIECES - LENT + i) * piece, piece)
        if hop == 0:
            src, dst, dev = wt_shard.at[span], via_in.at[i], (other, me)
        elif hop == 1:
            src, dst, dev = via_in.at[i], via_out.at[i], (sec, ahead(1))
        else:
            src, dst, dev = via_out.at[i], weight.at[ahead(1), span], (other, me)
        recv = w_recv.at[PIECES - LENT + i, 1] if hop == 2 else v_recv.at[hop, i]
        return remote(src, dst, v_send.at[hop, i], recv, dev)

    if lending:
        @pl.when(borrows)
        def _():
            for i in range(LENT):
                v_copy(0, i).start()

        @pl.when(lends)
        def _():
            for i in range(LENT + 1):
                if i < LENT:
                    v_copy(0, i).wait_recv()
                    v_copy(1, i).start()
                if i > 0:
                    v_copy(1, i - 1).wait_recv()
                    v_copy(2, i - 1).start()

    @pl.when(sec < top)
    def _():
        for p in direct:
            for d in range(1, chips):
                w_copy(p, 1, d, me, ahead(d), own=True).start()

        @pl.when(lone)
        def _():
            for p in lent:
                for d in range(1, chips):
                    w_copy(p, 1, d, me, ahead(d), own=True).start()

        for p in order:
            w_copy(p, 0, 0, me, pair, own=True).start()

    own_acts.wait()

    def prep(k, carry):
        x = acts[k].astype(f32)
        inv = lax.rsqrt(jnp.mean(x * x, -1, keepdims=True) + norm_eps)
        inv_rms[k] = inv
        for b in range(shards):
            cols = slice(b * blk, (b + 1) * blk)
            normed_own[b, k] = (acts[k, :, cols].astype(f32) * inv * gain[:, cols]).astype(bf16)
        @pl.when(sec < top)
        def _():
            normed_all[k, me] = normed_own[me, k]

        return carry

    lax.fori_loop(0, chunks, prep, 0)
    gain_acc[...] = jnp.zeros_like(gain_acc)
    total[...] = jnp.zeros_like(total)

    own_w.wait()

    def n_copy(d, src_slot, dst_slot):
        return remote(
            normed_own.at[src_slot], normed_all.at[:, dst_slot],
            n_send.at[d - 1], n_recv.at[d - 1], (sec, lax.rem(me + d, shards)),
        )

    @pl.when(sec < top)
    def _():
        for p in order:
            for d in range(1, chips):
                w_copy(p, 1, d, behind(d), ahead(d)).wait_recv()
                w_copy(p, 2, d, behind(d), pair).start()
        for p in range(PIECES):
            w_copy(p, 0, 0, pair, pair).wait_recv()
            for d in range(1, chips):
                w_copy(p, 2, d, behind(d, False), pair).wait_recv()
        for d in range(1, shards):
            n_copy(d, lax.rem(me + d, shards), me).start()

    batches, cands = labels.shape
    every = batches * cands
    per_batch = segs.shape[1] // rows
    classes = head.shape[1]
    quarter = width // 4

    def t_copy(n, src, dst, d):
        return remote(
            src, dst, t_send.at[n, d - 1], t_recv.at[n, d - 1], (sec, lax.rem(me + d, shards))
        )

    def sums_out(d):
        return t_copy(0, normed_all.at[0:2, lax.rem(me + d, shards), 0:every],
                      normed_all.at[2:4, me, 0:every], d)

    def parts_out(d):
        return t_copy(1, part_out.at[lax.rem(me + d, shards)], part_in.at[me], d)

    def logits_out(d):
        mine = grads.at[1, me, 0:every, 0:classes]
        return t_copy(2, mine, mine, d)

    def backs_out(d):
        return t_copy(3, normed_all.at[4, lax.rem(me + d, shards), 0:every],
                      normed_all.at[5, me, 0:every], d)

    def counts_out(d):
        mine = normed_all.at[6, me, 0:every, 0:128]
        return t_copy(4, mine, mine, d)

    def split(value):
        hi = value.astype(bf16)
        return hi, (value - hi.astype(f32)).astype(bf16)

    def flat(ref_value):
        return ref_value.reshape(shards * every, ref_value.shape[-1])

    @pl.when(is_top)
    def _():
        slots = lax.broadcasted_iota(jnp.int32, (every, rows), 0)
        counts = jnp.zeros((every, 1), f32)
        for k in range(chunks):
            m, at = k // per_batch, (k % per_batch) * rows
            hit = jnp.where(segs[m : m + 1, at : at + rows] + cands * m == slots, 1.0, 0.0)
            counts = counts + jnp.sum(hit, -1, keepdims=True)
            pool[k] = hit.astype(bf16)
        normed_all[6, me, 0:every, 0:128] = jnp.broadcast_to(counts, (every, 128)).astype(bf16)
        for b in range(shards):
            sums = jnp.zeros((every, blk), f32)
            for k in range(chunks):
                sums = sums + jnp.dot(pool[k], normed_own[b, k], preferred_element_type=f32)
            hi, lo = split(sums)
            normed_all[0, b, 0:every] = hi
            normed_all[1, b, 0:every] = lo
        for d in range(1, shards):
            sums_out(d).start()
        for d in range(1, shards):
            counts_out(d).start()
        normed_all[2, me, 0:every] = normed_all[0, me, 0:every]
        normed_all[3, me, 0:every] = normed_all[1, me, 0:every]
        own_head.wait()
        logits = jnp.zeros((2 * every, classes), f32)
        for b in range(4):
            cols = slice(b * quarter, (b + 1) * quarter)
            sums = jnp.zeros((every, quarter), f32)
            for k in range(chunks):
                sums = sums + jnp.dot(pool[k], acts[k, :, cols], preferred_element_type=f32)
            logits = logits + jnp.dot(
                jnp.concatenate(split(sums), 0), head[cols, :], preferred_element_type=f32
            )
        logits = logits[:every] + logits[every:]
        for d in range(1, shards):
            sums_out(d).wait_recv()
        both = jnp.concatenate([flat(normed_all[n, :, 0:every]) for n in (2, 3)], 0)
        part = jnp.zeros((shards * every, classes), f32)
        for b in range(4):
            cols = slice(b * quarter, (b + 1) * quarter)
            y = lax.dot_general(both, weight[me, cols, :], NT, preferred_element_type=f32)
            y = (y[: shards * every] + y[shards * every :]).astype(bf16)
            part = part + jnp.dot(y, head[cols, :], preferred_element_type=f32)
        part_out[...] = part.reshape(shards, every, classes)
        for d in range(1, shards):
            parts_out(d).start()
        part_in[me] = part_out[me]
        for d in range(1, shards):
            parts_out(d).wait_recv()
        logits = (logits + jnp.sum(part_in[...], 0)) / counts
        lanes = lax.broadcasted_iota(jnp.int32, (cands, cands), 1)
        diagonal = lanes == lax.broadcasted_iota(jnp.int32, (cands, cands), 0)
        target = []
        for m in range(batches):
            own = jnp.where(diagonal, labels[m : m + 1, :].astype(f32), 0.0)
            target.append(jnp.sum(own, -1, keepdims=True))
        target = jnp.concatenate(target, 0).astype(jnp.int32)
        target = lax.broadcasted_iota(jnp.int32, (every, classes), 1) == target
        dlogit = (jax.nn.sigmoid(logits) - jnp.where(target, 1.0, 0.0)).astype(bf16)
        grads[1, me, 0:every, 0:classes] = dlogit
        for d in range(1, shards):
            logits_out(d).start()
        for d in range(1, shards):
            counts_out(d).wait_recv()
        for d in range(1, shards):
            logits_out(d).wait_recv()
        all_counts = flat(normed_all[6, :, 0:every, 0:128])[:, 0:1].astype(f32)
        all_dlogit = flat(grads[1, :, 0:every, 0:classes])
        for b in range(4):
            cols = slice(b * quarter, (b + 1) * quarter)
            dpool = lax.dot_general(all_dlogit, head[cols, :], NT, preferred_element_type=f32)
            grads[0, :, 0:every, cols] = (
                (dpool / all_counts).astype(bf16).reshape(shards, every, quarter)
            )
        normed_all[4, :, 0:every] = (
            jnp.dot(flat(grads[0, :, 0:every]), weight[me], preferred_element_type=f32)
            .astype(bf16)
            .reshape(shards, every, blk)
        )
        for d in range(1, shards):
            backs_out(d).start()
        normed_all[5, me, 0:every] = normed_all[4, me, 0:every]
        for d in range(1, shards):
            backs_out(d).wait_recv()

    def c_copy(k):
        return remote(din.at[k], grads.at[k, me], c_send.at[k], c_recv.at[k], (sec - 1, me))

    def g_copy(k, kind, d, slot, target):
        n = 0 if kind == 0 else (d if kind == 1 else chips - 1 + d)
        return remote(
            grads.at[k, slot], grads.at[k, slot], g_send.at[k, n], g_recv.at[k, n], (sec, target)
        )

    def relay(k):
        for d in range(1, chips):
            g_copy(k, 1, d, behind(d), ahead(d)).wait_recv()
            g_copy(k, 2, d, behind(d), pair).start()

    def accumulate(k):
        g_copy(k, 0, 0, pair, pair).wait_recv()
        for d in range(1, chips):
            g_copy(k, 2, d, behind(d, False), pair).wait_recv()
        lhs = normed_all[k].reshape(shards * rows, blk)
        for b in range(4):
            cols = slice(b * (width // 4), (b + 1) * (width // 4))
            rhs = grads[k, :, :, cols].reshape(shards * rows, width // 4)
            total[:, cols] += lax.dot_general(lhs, rhs, TN, preferred_element_type=f32)

    lag = jnp.where(sec == 0, 1, jnp.clip(1 + 2 * (sec - (top - 4)), 3, chunks))

    def columns_here():
        for d in range(1, shards):
            n_copy(d, me, lax.rem(me + shards - d, shards)).wait_recv()

    def section_back(k, back_of, grad_of):
        inv = inv_rms[k]
        dots = jnp.zeros((rows, 1), f32)
        for b in range(shards):
            cols = slice(b * blk, (b + 1) * blk)
            back = back_of(b)
            back_s[:, cols] = back
            prod = back * (acts[k, :, cols].astype(f32) * inv)
            gain_acc[:, cols] += jnp.sum(prod, 0, keepdims=True)
            dots = dots + jnp.sum(prod * gain[:, cols], -1, keepdims=True)
        mean = dots / width
        for b in range(shards):
            cols = slice(b * blk, (b + 1) * blk)
            x_hat = acts[k, :, cols].astype(f32) * inv
            through = inv * (back_s[:, cols] * gain[:, cols] - x_hat * mean)
            din[k, :, cols] = (grad_of(cols) + through).astype(bf16)

        @pl.when(sec > 0)
        def _():
            c_copy(k).start()

    def top_step(k, carry):
        def pick(value):
            return lax.dot_general(pool[k], value, TN, preferred_element_type=f32)

        section_back(
            k,
            lambda b: pick(normed_all[5, b, 0:every]),
            lambda cols: pick(grads[0, me, 0:every, cols]),
        )
        return carry

    def step(k, carry):
        c_copy(k).wait_recv()
        g_copy(k, 0, 0, me, pair).start()
        for d in range(1, chips):
            g_copy(k, 1, d, me, ahead(d)).start()
        section_back(
            k,
            lambda b: jnp.dot(grads[k, me], weight[b], preferred_element_type=f32),
            lambda cols: grads[k, me, :, cols].astype(f32),
        )

        @pl.when(k >= lag)
        def _():
            relay(k - lag)

        @pl.when(k == lag + 1)
        def _():
            columns_here()

        @pl.when(k >= lag + 1)
        def _():
            accumulate(k - lag - 1)

        return carry

    @pl.when(is_top)
    def _():
        lax.fori_loop(0, chunks, top_step, 0)

    @pl.when(sec < top)
    def _():
        lax.fori_loop(0, chunks, step, 0)

    def d_copy(d, slot):
        return remote(
            gain_acc, gain_all.at[slot], d_send.at[d - 1], d_recv.at[d - 1],
            (sec, lax.rem(me + d, shards)),
        )

    for d in range(1, shards):
        d_copy(d, me).start()

    @pl.when(is_top)
    def _():
        every_grad = flat(grads[0, :, 0:every])
        for n in (2, 3):
            sums = flat(normed_all[n, :, 0:every])
            for b in range(4):
                cols = slice(b * quarter, (b + 1) * quarter)
                total[:, cols] += lax.dot_general(
                    sums, every_grad[:, cols], TN, preferred_element_type=f32
                )

    def relay_step(k, carry):
        relay(k)
        return carry

    def accumulate_step(k, carry):
        accumulate(k)
        return carry

    @pl.when(sec < top)
    def _():
        @pl.when(lag + 1 >= chunks)
        def _():
            columns_here()

        lax.fori_loop(chunks - lag, chunks, relay_step, 0)
        lax.fori_loop(jnp.maximum(chunks - lag - 1, 0), chunks, accumulate_step, 0)

    dproj[...] = total[...].astype(bf16)

    gain_all[me] = gain_acc[...]
    for d in range(1, shards):
        d_copy(d, lax.rem(me + shards - d, shards)).wait_recv()
    dgain[...] = jnp.sum(gain_all[...], 0)

    for d in range(1, shards):
        d_copy(d, me).wait_send()

    @pl.when(is_top)
    def _():
        for d in range(1, shards):
            sums_out(d).wait_send()
            counts_out(d).wait_send()
            parts_out(d).wait_send()
            logits_out(d).wait_send()
            backs_out(d).wait_send()

    @pl.when(sec < top)
    def _():
        for p in range(PIECES):
            w_copy(p, 0, 0, me, pair, own=True).wait_send()
            for d in range(1, chips):
                w_copy(p, 2, d, behind(d), pair).wait_send()
        for p in direct:
            for d in range(1, chips):
                w_copy(p, 1, d, me, ahead(d), own=True).wait_send()

        @pl.when(lone)
        def _():
            for p in lent:
                for d in range(1, chips):
                    w_copy(p, 1, d, me, ahead(d), own=True).wait_send()

        for d in range(1, shards):
            n_copy(d, lax.rem(me + d, shards), me).wait_send()

    if lending:
        @pl.when(borrows)
        def _():
            for i in range(LENT):
                v_copy(0, i).wait_send()

        @pl.when(lends)
        def _():
            for i in range(LENT):
                v_copy(1, i).wait_send()
                v_copy(2, i).wait_send()

    def sent(k, carry):
        @pl.when(sec > 0)
        def _():
            c_copy(k).wait_send()

        @pl.when(sec < top)
        def _():
            g_copy(k, 0, 0, me, pair).wait_send()
            for d in range(1, chips):
                g_copy(k, 1, d, me, ahead(d)).wait_send()
                g_copy(k, 2, d, behind(d), pair).wait_send()

        return carry

    lax.fori_loop(0, chunks, sent, 0)


def per_device(sections, shards, acts, gains, proj, head, segs, labels):
    tokens, width = acts.shape[1:]
    batches, rows = segs.shape
    cands = labels.shape[1]
    classes = head.shape[1]
    blk = proj.shape[1]
    chunks = tokens // CHUNK
    chips = shards // 2
    every = batches * cands
    vmem = pl.BlockSpec(memory_space=pltpu.VMEM)
    hbm = pl.BlockSpec(memory_space=pl.ANY)
    dma = pltpu.SemaphoreType.DMA
    din, dproj, dgain = pl.pallas_call(
        functools.partial(kernel, sections, shards, chunks),
        out_shape=(
            jax.ShapeDtypeStruct((chunks, CHUNK, width), bf16),
            jax.ShapeDtypeStruct((blk, width), bf16),
            jax.ShapeDtypeStruct((1, width), f32),
        ),
        in_specs=[hbm, vmem, hbm, hbm, vmem, vmem],
        out_specs=(vmem, vmem, vmem),
        scratch_shapes=[
            pltpu.VMEM((chunks, CHUNK, width), bf16),
            pltpu.VMEM((width, classes), bf16),
            pltpu.VMEM((shards, width, blk), bf16),
            pltpu.VMEM((chunks, shards, CHUNK, width), bf16),
            pltpu.VMEM((shards, chunks, CHUNK, blk), bf16),
            pltpu.VMEM((chunks, shards, CHUNK, blk), bf16),
            pltpu.VMEM((chunks, CHUNK, 1), f32),
            pltpu.VMEM((CHUNK, width), f32),
            pltpu.VMEM((blk, width), f32),
            pltpu.VMEM((1, width), f32),
            pltpu.VMEM((shards, 1, width), f32),
            pltpu.VMEM((chunks, every, CHUNK), bf16),
            pltpu.VMEM((shards, every, classes), f32),
            pltpu.VMEM((shards, every, classes), f32),
            pltpu.VMEM((LENT, width // PIECES if chips == 2 else 16, blk), bf16),
            pltpu.VMEM((LENT, width // PIECES if chips == 2 else 16, blk), bf16),
            dma((3,)),
            dma((PIECES, 2 * chips - 1)),
            dma((PIECES, 2 * chips - 1)),
            dma((shards - 1,)),
            dma((shards - 1,)),
            dma((chunks,)),
            dma((chunks,)),
            dma((chunks, 2 * chips - 1)),
            dma((chunks, 2 * chips - 1)),
            dma((shards - 1,)),
            dma((shards - 1,)),
            dma((5, shards - 1)),
            dma((5, shards - 1)),
            dma((3, LENT)),
            dma((3, LENT)),
        ],
        compiler_params=pltpu.CompilerParams(
            collective_id=0, has_side_effects=True, vmem_limit_bytes=127 * 512 * 1024
        ),
        cost_estimate=pl.CostEstimate(
            flops=4 * tokens * width * width, bytes_accessed=16 * width * width, transcendentals=0
        ),
    )(
        acts[0].reshape(chunks, CHUNK, width),
        gains,
        proj[0].T,
        head,
        segs,
        labels,
    )
    return din.reshape(1, tokens, width), dproj[None], dgain


def solution(mesh):
    return jax.shard_map(
        functools.partial(per_device, mesh.shape["section"], mesh.shape["fsdp"]),
        mesh=mesh,
        in_specs=(
            P("section", "fsdp", None),
            P("section", None),
            P("section", "fsdp", None),
            P(),
            P("fsdp", None),
            P("fsdp", None),
        ),
        out_specs=(P("section", "fsdp", None), P("section", "fsdp", None), P("section", None)),
        check_vma=False,
    )
```

```python
import functools

import jax
import jax.numpy as jnp
from jax import lax
from jax.experimental import pallas as pl
from jax.experimental.pallas import tpu as pltpu
from jax.sharding import PartitionSpec as P

norm_eps = 1e-06
MESH = pl.DeviceIdType.MESH
CHUNK = 48
PIECES = 16
LENT = 5
bf16, f32 = jnp.bfloat16, jnp.float32
NT = (((1,), (1,)), ((), ()))
TN = (((0,), (0,)), ((), ()))


def kernel(
    sections, shards, chunks,
    acts_hbm, gain, wt_shard, head_hbm, segs, labels,
    din, dproj, dgain,
    acts, head, weight, grads, normed_own, normed_all, inv_rms, back_s, total, gain_acc, gain_all,
    pool, part_out, part_in, via_in, via_out,
    local_sem, w_send, w_recv, n_send, n_recv, c_send, c_recv, g_send, g_recv, d_send, d_recv,
    t_send, t_recv, v_send, v_recv,
):
    sec = lax.axis_index("section")
    me = lax.axis_index("fsdp")
    top = sections - 1
    chips = shards // 2
    chip, core = me // 2, lax.rem(me, 2)
    pair = chip * 2 + 1 - core
    width = gain.shape[1]
    blk = width // shards
    rows = CHUNK
    is_top = sec == top
    lending = chips == 2 and sections >= 8
    other = top - 1 - sec
    borrows = jnp.logical_and(lending, jnp.logical_and(sec >= top - 2, sec < top))
    lends = jnp.logical_and(lending, sec <= 1)
    lone = jnp.logical_not(borrows)
    direct = list(range(PIECES - LENT))
    lent = list(range(PIECES - LENT, PIECES))
    order = [p for i in direct for p in (direct[i : i + 1] + lent[i : i + 1])]

    def ahead(d):
        return lax.rem(chip + d, chips) * 2 + core

    def behind(d, own_core=True):
        return lax.rem(chip + chips - d, chips) * 2 + (core if own_core else 1 - core)

    own_acts = pltpu.make_async_copy(acts_hbm, acts, local_sem.at[1])
    own_acts.start()
    own_w = pltpu.make_async_copy(wt_shard, weight.at[me], local_sem.at[0])
    own_w.start()
    own_head = pltpu.make_async_copy(head_hbm, head, local_sem.at[2])

    @pl.when(is_top)
    def _():
        own_head.start()

    barrier = pltpu.get_barrier_semaphore()
    for d in range(1, shards):
        pl.semaphore_signal(barrier, 1, device_id=(sec, lax.rem(me + d, shards)), device_id_type=MESH)

    @pl.when(sec > 0)
    def _():
        pl.semaphore_signal(barrier, 1, device_id=(sec - 1, me), device_id_type=MESH)

    @pl.when(sec < top)
    def _():
        pl.semaphore_signal(barrier, 1, device_id=(sec + 1, me), device_id_type=MESH)

    @pl.when(jnp.logical_or(borrows, lends))
    def _():
        pl.semaphore_signal(barrier, 1, device_id=(other, me), device_id_type=MESH)

    pl.semaphore_wait(
        barrier,
        shards - 1
        + jnp.where(sec > 0, 1, 0)
        + jnp.where(sec < top, 1, 0)
        + jnp.where(jnp.logical_or(borrows, lends), 1, 0),
    )

    def remote(src, dst, send, recv, dev):
        return pltpu.make_async_remote_copy(
            src_ref=src, dst_ref=dst, send_sem=send, recv_sem=recv,
            device_id=dev, device_id_type=MESH,
        )

    piece = width // PIECES

    def w_copy(p, kind, d, src_slot, target, own=False):
        span = pl.ds(p * piece, piece)
        n = 0 if kind == 0 else (d if kind == 1 else chips - 1 + d)
        src = wt_shard.at[span] if own else weight.at[src_slot, span]
        return remote(src, weight.at[src_slot, span], w_send.at[p, n], w_recv.at[p, n], (sec, target))

    def v_copy(hop, i):
        span = pl.ds((PIECES - LENT + i) * piece, piece)
        if hop == 0:
            src, dst, dev = wt_shard.at[span], via_in.at[i], (other, me)
        elif hop == 1:
            src, dst, dev = via_in.at[i], via_out.at[i], (sec, ahead(1))
        else:
            src, dst, dev = via_out.at[i], weight.at[ahead(1), span], (other, me)
        recv = w_recv.at[PIECES - LENT + i, 1] if hop == 2 else v_recv.at[hop, i]
        return remote(src, dst, v_send.at[hop, i], recv, dev)

    if lending:
        @pl.when(borrows)
        def _():
            for i in range(LENT):
                v_copy(0, i).start()

        @pl.when(lends)
        def _():
            for i in range(LENT + 1):
                if i < LENT:
                    v_copy(0, i).wait_recv()
                    v_copy(1, i).start()
                if i > 0:
                    v_copy(1, i - 1).wait_recv()
                    v_copy(2, i - 1).start()

    @pl.when(sec < top)
    def _():
        for p in direct:
            for d in range(1, chips):
                w_copy(p, 1, d, me, ahead(d), own=True).start()

        @pl.when(lone)
        def _():
            for p in lent:
                for d in range(1, chips):
                    w_copy(p, 1, d, me, ahead(d), own=True).start()

        for p in order:
            w_copy(p, 0, 0, me, pair, own=True).start()

    own_acts.wait()

    def prep(k, carry):
        x = acts[k].astype(f32)
        inv = lax.rsqrt(jnp.mean(x * x, -1, keepdims=True) + norm_eps)
        inv_rms[k] = inv
        for b in range(shards):
            cols = slice(b * blk, (b + 1) * blk)
            normed_own[b, k] = (acts[k, :, cols].astype(f32) * inv * gain[:, cols]).astype(bf16)
        @pl.when(sec < top)
        def _():
            normed_all[k, me] = normed_own[me, k]

        return carry

    lax.fori_loop(0, chunks, prep, 0)
    gain_acc[...] = jnp.zeros_like(gain_acc)
    total[...] = jnp.zeros_like(total)

    own_w.wait()

    def n_copy(d, src_slot, dst_slot):
        return remote(
            normed_own.at[src_slot], normed_all.at[:, dst_slot],
            n_send.at[d - 1], n_recv.at[d - 1], (sec, lax.rem(me + d, shards)),
        )

    @pl.when(sec < top)
    def _():
        for p in order:
            for d in range(1, chips):
                w_copy(p, 1, d, behind(d), ahead(d)).wait_recv()
                w_copy(p, 2, d, behind(d), pair).start()
        for p in range(PIECES):
            w_copy(p, 0, 0, pair, pair).wait_recv()
            for d in range(1, chips):
                w_copy(p, 2, d, behind(d, False), pair).wait_recv()
        for d in range(1, shards):
            n_copy(d, lax.rem(me + d, shards), me).start()

    batches, cands = labels.shape
    every = batches * cands
    per_batch = segs.shape[1] // rows
    classes = head.shape[1]
    quarter = width // 4

    def t_copy(n, src, dst, d):
        return remote(
            src, dst, t_send.at[n, d - 1], t_recv.at[n, d - 1], (sec, lax.rem(me + d, shards))
        )

    def sums_out(d):
        return t_copy(0, normed_all.at[0:2, lax.rem(me + d, shards), 0:every],
                      normed_all.at[2:4, me, 0:every], d)

    def parts_out(d):
        return t_copy(1, part_out.at[lax.rem(me + d, shards)], part_in.at[me], d)

    def logits_out(d):
        mine = grads.at[1, me, 0:every, 0:classes]
        return t_copy(2, mine, mine, d)

    def backs_out(d):
        return t_copy(3, normed_all.at[4, lax.rem(me + d, shards), 0:every],
                      normed_all.at[5, me, 0:every], d)

    def counts_out(d):
        mine = normed_all.at[6, me, 0:every, 0:128]
        return t_copy(4, mine, mine, d)

    def split(value):
        hi = value.astype(bf16)
        return hi, (value - hi.astype(f32)).astype(bf16)

    def flat(ref_value):
        return ref_value.reshape(shards * every, ref_value.shape[-1])

    @pl.when(is_top)
    def _():
        slots = lax.broadcasted_iota(jnp.int32, (every, rows), 0)
        counts = jnp.zeros((every, 1), f32)
        for k in range(chunks):
            m, at = k // per_batch, (k % per_batch) * rows
            hit = jnp.where(segs[m : m + 1, at : at + rows] + cands * m == slots, 1.0, 0.0)
            counts = counts + jnp.sum(hit, -1, keepdims=True)
            pool[k] = hit.astype(bf16)
        normed_all[6, me, 0:every, 0:128] = jnp.broadcast_to(counts, (every, 128)).astype(bf16)
        for b in range(shards):
            sums = jnp.zeros((every, blk), f32)
            for k in range(chunks):
                sums = sums + jnp.dot(pool[k], normed_own[b, k], preferred_element_type=f32)
            hi, lo = split(sums)
            normed_all[0, b, 0:every] = hi
            normed_all[1, b, 0:every] = lo
        for d in range(1, shards):
            sums_out(d).start()
        for d in range(1, shards):
            counts_out(d).start()
        normed_all[2, me, 0:every] = normed_all[0, me, 0:every]
        normed_all[3, me, 0:every] = normed_all[1, me, 0:every]
        own_head.wait()
        logits = jnp.zeros((2 * every, classes), f32)
        for b in range(4):
            cols = slice(b * quarter, (b + 1) * quarter)
            sums = jnp.zeros((every, quarter), f32)
            for k in range(chunks):
                sums = sums + jnp.dot(pool[k], acts[k, :, cols], preferred_element_type=f32)
            logits = logits + jnp.dot(
                jnp.concatenate(split(sums), 0), head[cols, :], preferred_element_type=f32
            )
        logits = logits[:every] + logits[every:]
        for d in range(1, shards):
            sums_out(d).wait_recv()
        both = jnp.concatenate([flat(normed_all[n, :, 0:every]) for n in (2, 3)], 0)
        part = jnp.zeros((shards * every, classes), f32)
        for b in range(4):
            cols = slice(b * quarter, (b + 1) * quarter)
            y = lax.dot_general(both, weight[me, cols, :], NT, preferred_element_type=f32)
            y = (y[: shards * every] + y[shards * every :]).astype(bf16)
            part = part + jnp.dot(y, head[cols, :], preferred_element_type=f32)
        part_out[...] = part.reshape(shards, every, classes)
        for d in range(1, shards):
            parts_out(d).start()
        part_in[me] = part_out[me]
        for d in range(1, shards):
            parts_out(d).wait_recv()
        logits = (logits + jnp.sum(part_in[...], 0)) / counts
        lanes = lax.broadcasted_iota(jnp.int32, (cands, cands), 1)
        diagonal = lanes == lax.broadcasted_iota(jnp.int32, (cands, cands), 0)
        target = []
        for m in range(batches):
            own = jnp.where(diagonal, labels[m : m + 1, :].astype(f32), 0.0)
            target.append(jnp.sum(own, -1, keepdims=True))
        target = jnp.concatenate(target, 0).astype(jnp.int32)
        target = lax.broadcasted_iota(jnp.int32, (every, classes), 1) == target
        dlogit = (jax.nn.sigmoid(logits) - jnp.where(target, 1.0, 0.0)).astype(bf16)
        grads[1, me, 0:every, 0:classes] = dlogit
        for d in range(1, shards):
            logits_out(d).start()
        for d in range(1, shards):
            counts_out(d).wait_recv()
        for d in range(1, shards):
            logits_out(d).wait_recv()
        all_counts = flat(normed_all[6, :, 0:every, 0:128])[:, 0:1].astype(f32)
        all_dlogit = flat(grads[1, :, 0:every, 0:classes])
        for b in range(4):
            cols = slice(b * quarter, (b + 1) * quarter)
            dpool = lax.dot_general(all_dlogit, head[cols, :], NT, preferred_element_type=f32)
            grads[0, :, 0:every, cols] = (
                (dpool / all_counts).astype(bf16).reshape(shards, every, quarter)
            )
        normed_all[4, :, 0:every] = (
            jnp.dot(flat(grads[0, :, 0:every]), weight[me], preferred_element_type=f32)
            .astype(bf16)
            .reshape(shards, every, blk)
        )
        for d in range(1, shards):
            backs_out(d).start()
        normed_all[5, me, 0:every] = normed_all[4, me, 0:every]
        for d in range(1, shards):
            backs_out(d).wait_recv()

    def c_copy(k):
        return remote(din.at[k], grads.at[k, me], c_send.at[k], c_recv.at[k], (sec - 1, me))

    def g_copy(k, kind, d, slot, target):
        n = 0 if kind == 0 else (d if kind == 1 else chips - 1 + d)
        return remote(
            grads.at[k, slot], grads.at[k, slot], g_send.at[k, n], g_recv.at[k, n], (sec, target)
        )

    def relay(k):
        for d in range(1, chips):
            g_copy(k, 1, d, behind(d), ahead(d)).wait_recv()
            g_copy(k, 2, d, behind(d), pair).start()

    def accumulate(k, last=False):
        g_copy(k, 0, 0, pair, pair).wait_recv()
        for d in range(1, chips):
            g_copy(k, 2, d, behind(d, False), pair).wait_recv()
        lhs = normed_all[k].reshape(shards * rows, blk)
        for b in range(4):
            cols = slice(b * (width // 4), (b + 1) * (width // 4))
            rhs = grads[k, :, :, cols].reshape(shards * rows, width // 4)
            term = lax.dot_general(lhs, rhs, TN, preferred_element_type=f32)
            if last:
                dproj[:, cols] = (total[:, cols] + term).astype(bf16)
            else:
                total[:, cols] += term

    lag = jnp.where(sec == 0, 1, jnp.clip(2 + 3 * (sec - (top - 4)), 4, chunks - 1))

    def columns_here():
        for d in range(1, shards):
            n_copy(d, me, lax.rem(me + shards - d, shards)).wait_recv()

    def section_back(k, back_of, grad_of):
        inv = inv_rms[k]
        dots = jnp.zeros((rows, 1), f32)
        for b in range(shards):
            cols = slice(b * blk, (b + 1) * blk)
            back = back_of(b)
            back_s[:, cols] = back
            prod = back * (acts[k, :, cols].astype(f32) * inv)
            gain_acc[:, cols] += jnp.sum(prod, 0, keepdims=True)
            dots = dots + jnp.sum(prod * gain[:, cols], -1, keepdims=True)
        mean = dots / width
        for b in range(shards):
            cols = slice(b * blk, (b + 1) * blk)
            x_hat = acts[k, :, cols].astype(f32) * inv
            through = inv * (back_s[:, cols] * gain[:, cols] - x_hat * mean)
            din[k, :, cols] = (grad_of(cols) + through).astype(bf16)

        @pl.when(sec > 0)
        def _():
            c_copy(k).start()

    def top_step(k, carry):
        def pick(value):
            return lax.dot_general(pool[k], value, TN, preferred_element_type=f32)

        section_back(
            k,
            lambda b: pick(normed_all[5, b, 0:every]),
            lambda cols: pick(grads[0, me, 0:every, cols]),
        )
        return carry

    def step(k, carry):
        c_copy(k).wait_recv()
        g_copy(k, 0, 0, me, pair).start()
        for d in range(1, chips):
            g_copy(k, 1, d, me, ahead(d)).start()
        section_back(
            k,
            lambda b: jnp.dot(grads[k, me], weight[b], preferred_element_type=f32),
            lambda cols: grads[k, me, :, cols].astype(f32),
        )

        @pl.when(k >= lag)
        def _():
            relay(k - lag)

        @pl.when(k == lag + 1)
        def _():
            columns_here()

        @pl.when(k >= lag + 1)
        def _():
            accumulate(k - lag - 1)

        return carry

    @pl.when(is_top)
    def _():
        lax.fori_loop(0, chunks, top_step, 0)

    @pl.when(sec < top)
    def _():
        lax.fori_loop(0, chunks, step, 0)

    def d_copy(d, slot):
        return remote(
            gain_acc, gain_all.at[slot], d_send.at[d - 1], d_recv.at[d - 1],
            (sec, lax.rem(me + d, shards)),
        )

    for d in range(1, shards):
        d_copy(d, me).start()

    @pl.when(is_top)
    def _():
        every_grad = flat(grads[0, :, 0:every])
        for n in (2, 3):
            sums = flat(normed_all[n, :, 0:every])
            for b in range(4):
                cols = slice(b * quarter, (b + 1) * quarter)
                total[:, cols] += lax.dot_general(
                    sums, every_grad[:, cols], TN, preferred_element_type=f32
                )
        dproj[...] = total[...].astype(bf16)

    def catch_up(k, carry):
        accumulate(k - 1)
        relay(k)
        return carry

    @pl.when(sec < top)
    def _():
        @pl.when(lag + 1 >= chunks)
        def _():
            columns_here()

        lax.fori_loop(chunks - lag, chunks, catch_up, 0)
        accumulate(chunks - 1, last=True)

    gain_all[me] = gain_acc[...]
    for d in range(1, shards):
        d_copy(d, lax.rem(me + shards - d, shards)).wait_recv()
    dgain[...] = jnp.sum(gain_all[...], 0)

    for d in range(1, shards):
        d_copy(d, me).wait_send()

    @pl.when(is_top)
    def _():
        for d in range(1, shards):
            sums_out(d).wait_send()
            counts_out(d).wait_send()
            parts_out(d).wait_send()
            logits_out(d).wait_send()
            backs_out(d).wait_send()

    @pl.when(sec < top)
    def _():
        for p in range(PIECES):
            w_copy(p, 0, 0, me, pair, own=True).wait_send()
            for d in range(1, chips):
                w_copy(p, 2, d, behind(d), pair).wait_send()
        for p in direct:
            for d in range(1, chips):
                w_copy(p, 1, d, me, ahead(d), own=True).wait_send()

        @pl.when(lone)
        def _():
            for p in lent:
                for d in range(1, chips):
                    w_copy(p, 1, d, me, ahead(d), own=True).wait_send()

        for d in range(1, shards):
            n_copy(d, lax.rem(me + d, shards), me).wait_send()

    if lending:
        @pl.when(borrows)
        def _():
            for i in range(LENT):
                v_copy(0, i).wait_send()

        @pl.when(lends)
        def _():
            for i in range(LENT):
                v_copy(1, i).wait_send()
                v_copy(2, i).wait_send()

    def sent(k, carry):
        @pl.when(sec > 0)
        def _():
            c_copy(k).wait_send()

        @pl.when(sec < top)
        def _():
            g_copy(k, 0, 0, me, pair).wait_send()
            for d in range(1, chips):
                g_copy(k, 1, d, me, ahead(d)).wait_send()
                g_copy(k, 2, d, behind(d), pair).wait_send()

        return carry

    lax.fori_loop(0, chunks, sent, 0)


def per_device(sections, shards, acts, gains, proj, head, segs, labels):
    tokens, width = acts.shape[1:]
    batches, rows = segs.shape
    cands = labels.shape[1]
    classes = head.shape[1]
    blk = proj.shape[1]
    chunks = tokens // CHUNK
    chips = shards // 2
    every = batches * cands
    vmem = pl.BlockSpec(memory_space=pltpu.VMEM)
    hbm = pl.BlockSpec(memory_space=pl.ANY)
    dma = pltpu.SemaphoreType.DMA
    din, dproj, dgain = pl.pallas_call(
        functools.partial(kernel, sections, shards, chunks),
        out_shape=(
            jax.ShapeDtypeStruct((chunks, CHUNK, width), bf16),
            jax.ShapeDtypeStruct((blk, width), bf16),
            jax.ShapeDtypeStruct((1, width), f32),
        ),
        in_specs=[hbm, vmem, hbm, hbm, vmem, vmem],
        out_specs=(vmem, vmem, vmem),
        scratch_shapes=[
            pltpu.VMEM((chunks, CHUNK, width), bf16),
            pltpu.VMEM((width, classes), bf16),
            pltpu.VMEM((shards, width, blk), bf16),
            pltpu.VMEM((chunks, shards, CHUNK, width), bf16),
            pltpu.VMEM((shards, chunks, CHUNK, blk), bf16),
            pltpu.VMEM((chunks, shards, CHUNK, blk), bf16),
            pltpu.VMEM((chunks, CHUNK, 1), f32),
            pltpu.VMEM((CHUNK, width), f32),
            pltpu.VMEM((blk, width), f32),
            pltpu.VMEM((1, width), f32),
            pltpu.VMEM((shards, 1, width), f32),
            pltpu.VMEM((chunks, every, CHUNK), bf16),
            pltpu.VMEM((shards, every, classes), f32),
            pltpu.VMEM((shards, every, classes), f32),
            pltpu.VMEM((LENT, width // PIECES if chips == 2 else 16, blk), bf16),
            pltpu.VMEM((LENT, width // PIECES if chips == 2 else 16, blk), bf16),
            dma((3,)),
            dma((PIECES, 2 * chips - 1)),
            dma((PIECES, 2 * chips - 1)),
            dma((shards - 1,)),
            dma((shards - 1,)),
            dma((chunks,)),
            dma((chunks,)),
            dma((chunks, 2 * chips - 1)),
            dma((chunks, 2 * chips - 1)),
            dma((shards - 1,)),
            dma((shards - 1,)),
            dma((5, shards - 1)),
            dma((5, shards - 1)),
            dma((3, LENT)),
            dma((3, LENT)),
        ],
        compiler_params=pltpu.CompilerParams(
            collective_id=0, has_side_effects=True, vmem_limit_bytes=127 * 512 * 1024
        ),
        cost_estimate=pl.CostEstimate(
            flops=4 * tokens * width * width, bytes_accessed=16 * width * width, transcendentals=0
        ),
    )(
        acts[0].reshape(chunks, CHUNK, width),
        gains,
        proj[0].T,
        head,
        segs,
        labels,
    )
    return din.reshape(1, tokens, width), dproj[None], dgain


def solution(mesh):
    return jax.shard_map(
        functools.partial(per_device, mesh.shape["section"], mesh.shape["fsdp"]),
        mesh=mesh,
        in_specs=(
            P("section", "fsdp", None),
            P("section", None),
            P("section", "fsdp", None),
            P(),
            P("fsdp", None),
            P("fsdp", None),
        ),
        out_specs=(P("section", "fsdp", None), P("section", "fsdp", None), P("section", None)),
        check_vma=False,
    )
```

```python
import functools

import jax
import jax.numpy as jnp
from jax import lax
from jax.experimental import pallas as pl
from jax.experimental.pallas import tpu as pltpu
from jax.sharding import PartitionSpec as P

norm_eps = 1e-06
MESH = pl.DeviceIdType.MESH
CHUNK = 48
PIECES = 16
LENT = 3
bf16, f32 = jnp.bfloat16, jnp.float32
NT = (((1,), (1,)), ((), ()))
TN = (((0,), (0,)), ((), ()))


def kernel(
    sections, shards, chunks,
    acts_hbm, gain, wt_shard, head_hbm, segs, labels,
    din, dproj, dgain,
    acts, head, weight, grads, normed_own, normed_all, inv_rms, back_s, total, gain_acc, gain_all,
    pool, part_out, part_in, via_in, via_out,
    local_sem, w_send, w_recv, n_send, n_recv, c_send, c_recv, g_send, g_recv, d_send, d_recv,
    t_send, t_recv, v_send, v_recv,
):
    sec = lax.axis_index("section")
    me = lax.axis_index("fsdp")
    top = sections - 1
    chips = shards // 2
    chip, core = me // 2, lax.rem(me, 2)
    pair = chip * 2 + 1 - core
    width = gain.shape[1]
    blk = width // shards
    rows = CHUNK
    is_top = sec == top
    lending = chips == 2 and sections >= 8
    other = top - 1 - sec
    borrows = jnp.logical_and(lending, jnp.logical_and(sec >= top - 2, sec < top))
    lends = jnp.logical_and(lending, sec <= 1)
    lone = jnp.logical_not(borrows)
    direct = list(range(PIECES - LENT))
    lent = list(range(PIECES - LENT, PIECES))
    order = [p for i in direct for p in (direct[i : i + 1] + lent[i : i + 1])]

    def ahead(d):
        return lax.rem(chip + d, chips) * 2 + core

    def behind(d, own_core=True):
        return lax.rem(chip + chips - d, chips) * 2 + (core if own_core else 1 - core)

    own_acts = pltpu.make_async_copy(acts_hbm, acts, local_sem.at[1])
    own_acts.start()
    own_w = pltpu.make_async_copy(wt_shard, weight.at[me], local_sem.at[0])
    own_w.start()
    own_head = pltpu.make_async_copy(head_hbm, head, local_sem.at[2])

    @pl.when(is_top)
    def _():
        own_head.start()

    barrier = pltpu.get_barrier_semaphore()
    for d in range(1, shards):
        pl.semaphore_signal(barrier, 1, device_id=(sec, lax.rem(me + d, shards)), device_id_type=MESH)

    @pl.when(sec > 0)
    def _():
        pl.semaphore_signal(barrier, 1, device_id=(sec - 1, me), device_id_type=MESH)

    @pl.when(sec < top)
    def _():
        pl.semaphore_signal(barrier, 1, device_id=(sec + 1, me), device_id_type=MESH)

    @pl.when(jnp.logical_or(borrows, lends))
    def _():
        pl.semaphore_signal(barrier, 1, device_id=(other, me), device_id_type=MESH)

    pl.semaphore_wait(
        barrier,
        shards - 1
        + jnp.where(sec > 0, 1, 0)
        + jnp.where(sec < top, 1, 0)
        + jnp.where(jnp.logical_or(borrows, lends), 1, 0),
    )

    def remote(src, dst, send, recv, dev):
        return pltpu.make_async_remote_copy(
            src_ref=src, dst_ref=dst, send_sem=send, recv_sem=recv,
            device_id=dev, device_id_type=MESH,
        )

    piece = width // PIECES

    def w_copy(p, kind, d, src_slot, target, own=False):
        span = pl.ds(p * piece, piece)
        n = 0 if kind == 0 else (d if kind == 1 else chips - 1 + d)
        src = wt_shard.at[span] if own else weight.at[src_slot, span]
        return remote(src, weight.at[src_slot, span], w_send.at[p, n], w_recv.at[p, n], (sec, target))

    def v_copy(hop, i):
        span = pl.ds((PIECES - LENT + i) * piece, piece)
        if hop == 0:
            src, dst, dev = wt_shard.at[span], via_in.at[i], (other, me)
        elif hop == 1:
            src, dst, dev = via_in.at[i], via_out.at[i], (sec, ahead(1))
        else:
            src, dst, dev = via_out.at[i], weight.at[ahead(1), span], (other, me)
        recv = w_recv.at[PIECES - LENT + i, 1] if hop == 2 else v_recv.at[hop, i]
        return remote(src, dst, v_send.at[hop, i], recv, dev)

    if lending:
        @pl.when(borrows)
        def _():
            for i in range(LENT):
                v_copy(0, i).start()

        @pl.when(lends)
        def _():
            for i in range(LENT + 1):
                if i < LENT:
                    v_copy(0, i).wait_recv()
                    v_copy(1, i).start()
                if i > 0:
                    v_copy(1, i - 1).wait_recv()
                    v_copy(2, i - 1).start()

    @pl.when(sec < top)
    def _():
        for p in direct:
            for d in range(1, chips):
                w_copy(p, 1, d, me, ahead(d), own=True).start()

        @pl.when(lone)
        def _():
            for p in lent:
                for d in range(1, chips):
                    w_copy(p, 1, d, me, ahead(d), own=True).start()

        for p in order:
            w_copy(p, 0, 0, me, pair, own=True).start()

    own_acts.wait()

    def prep(k, carry):
        x = acts[k].astype(f32)
        inv = lax.rsqrt(jnp.mean(x * x, -1, keepdims=True) + norm_eps)
        inv_rms[k] = inv
        for b in range(shards):
            cols = slice(b * blk, (b + 1) * blk)
            normed_own[b, k] = (acts[k, :, cols].astype(f32) * inv * gain[:, cols]).astype(bf16)
        @pl.when(sec < top)
        def _():
            normed_all[k, me] = normed_own[me, k]

        return carry

    lax.fori_loop(0, chunks, prep, 0)
    gain_acc[...] = jnp.zeros_like(gain_acc)
    total[...] = jnp.zeros_like(total)

    own_w.wait()

    def n_copy(d, src_slot, dst_slot):
        return remote(
            normed_own.at[src_slot], normed_all.at[:, dst_slot],
            n_send.at[d - 1], n_recv.at[d - 1], (sec, lax.rem(me + d, shards)),
        )

    @pl.when(sec < top)
    def _():
        for p in order:
            for d in range(1, chips):
                w_copy(p, 1, d, behind(d), ahead(d)).wait_recv()
                w_copy(p, 2, d, behind(d), pair).start()
        for p in range(PIECES):
            w_copy(p, 0, 0, pair, pair).wait_recv()
            for d in range(1, chips):
                w_copy(p, 2, d, behind(d, False), pair).wait_recv()
        for d in range(1, shards):
            n_copy(d, lax.rem(me + d, shards), me).start()

    batches, cands = labels.shape
    every = batches * cands
    per_batch = segs.shape[1] // rows
    classes = head.shape[1]
    quarter = width // 4

    def t_copy(n, src, dst, d):
        return remote(
            src, dst, t_send.at[n, d - 1], t_recv.at[n, d - 1], (sec, lax.rem(me + d, shards))
        )

    def sums_out(d):
        return t_copy(0, normed_all.at[0:2, lax.rem(me + d, shards), 0:every],
                      normed_all.at[2:4, me, 0:every], d)

    def parts_out(d):
        return t_copy(1, part_out.at[lax.rem(me + d, shards)], part_in.at[me], d)

    def logits_out(d):
        mine = grads.at[1, me, 0:every, 0:classes]
        return t_copy(2, mine, mine, d)

    def backs_out(d):
        return t_copy(3, normed_all.at[4, lax.rem(me + d, shards), 0:every],
                      normed_all.at[5, me, 0:every], d)

    def counts_out(d):
        mine = normed_all.at[6, me, 0:every, 0:128]
        return t_copy(4, mine, mine, d)

    def split(value):
        hi = value.astype(bf16)
        return hi, (value - hi.astype(f32)).astype(bf16)

    def flat(ref_value):
        return ref_value.reshape(shards * every, ref_value.shape[-1])

    @pl.when(is_top)
    def _():
        slots = lax.broadcasted_iota(jnp.int32, (every, rows), 0)
        counts = jnp.zeros((every, 1), f32)
        for k in range(chunks):
            m, at = k // per_batch, (k % per_batch) * rows
            hit = jnp.where(segs[m : m + 1, at : at + rows] + cands * m == slots, 1.0, 0.0)
            counts = counts + jnp.sum(hit, -1, keepdims=True)
            pool[k] = hit.astype(bf16)
        normed_all[6, me, 0:every, 0:128] = jnp.broadcast_to(counts, (every, 128)).astype(bf16)
        for b in range(shards):
            sums = jnp.zeros((every, blk), f32)
            for k in range(chunks):
                sums = sums + jnp.dot(pool[k], normed_own[b, k], preferred_element_type=f32)
            hi, lo = split(sums)
            normed_all[0, b, 0:every] = hi
            normed_all[1, b, 0:every] = lo
        for d in range(1, shards):
            sums_out(d).start()
        for d in range(1, shards):
            counts_out(d).start()
        normed_all[2, me, 0:every] = normed_all[0, me, 0:every]
        normed_all[3, me, 0:every] = normed_all[1, me, 0:every]
        own_head.wait()
        logits = jnp.zeros((2 * every, classes), f32)
        for b in range(4):
            cols = slice(b * quarter, (b + 1) * quarter)
            sums = jnp.zeros((every, quarter), f32)
            for k in range(chunks):
                sums = sums + jnp.dot(pool[k], acts[k, :, cols], preferred_element_type=f32)
            logits = logits + jnp.dot(
                jnp.concatenate(split(sums), 0), head[cols, :], preferred_element_type=f32
            )
        logits = logits[:every] + logits[every:]
        for d in range(1, shards):
            sums_out(d).wait_recv()
        both = jnp.concatenate([flat(normed_all[n, :, 0:every]) for n in (2, 3)], 0)
        part = jnp.zeros((shards * every, classes), f32)
        for b in range(4):
            cols = slice(b * quarter, (b + 1) * quarter)
            y = lax.dot_general(both, weight[me, cols, :], NT, preferred_element_type=f32)
            y = (y[: shards * every] + y[shards * every :]).astype(bf16)
            part = part + jnp.dot(y, head[cols, :], preferred_element_type=f32)
        part_out[...] = part.reshape(shards, every, classes)
        for d in range(1, shards):
            parts_out(d).start()
        part_in[me] = part_out[me]
        for d in range(1, shards):
            parts_out(d).wait_recv()
        logits = (logits + jnp.sum(part_in[...], 0)) / counts
        lanes = lax.broadcasted_iota(jnp.int32, (cands, cands), 1)
        diagonal = lanes == lax.broadcasted_iota(jnp.int32, (cands, cands), 0)
        target = []
        for m in range(batches):
            own = jnp.where(diagonal, labels[m : m + 1, :].astype(f32), 0.0)
            target.append(jnp.sum(own, -1, keepdims=True))
        target = jnp.concatenate(target, 0).astype(jnp.int32)
        target = lax.broadcasted_iota(jnp.int32, (every, classes), 1) == target
        dlogit = (jax.nn.sigmoid(logits) - jnp.where(target, 1.0, 0.0)).astype(bf16)
        grads[1, me, 0:every, 0:classes] = dlogit
        for d in range(1, shards):
            logits_out(d).start()
        for d in range(1, shards):
            counts_out(d).wait_recv()
        for d in range(1, shards):
            logits_out(d).wait_recv()
        all_counts = flat(normed_all[6, :, 0:every, 0:128])[:, 0:1].astype(f32)
        all_dlogit = flat(grads[1, :, 0:every, 0:classes])
        for b in range(4):
            cols = slice(b * quarter, (b + 1) * quarter)
            dpool = lax.dot_general(all_dlogit, head[cols, :], NT, preferred_element_type=f32)
            grads[0, :, 0:every, cols] = (
                (dpool / all_counts).astype(bf16).reshape(shards, every, quarter)
            )
        normed_all[4, :, 0:every] = (
            jnp.dot(flat(grads[0, :, 0:every]), weight[me], preferred_element_type=f32)
            .astype(bf16)
            .reshape(shards, every, blk)
        )
        for d in range(1, shards):
            backs_out(d).start()
        normed_all[5, me, 0:every] = normed_all[4, me, 0:every]
        for d in range(1, shards):
            backs_out(d).wait_recv()

    def c_copy(k):
        return remote(din.at[k], grads.at[k, me], c_send.at[k], c_recv.at[k], (sec - 1, me))

    def g_copy(k, kind, d, slot, target):
        n = 0 if kind == 0 else (d if kind == 1 else chips - 1 + d)
        return remote(
            grads.at[k, slot], grads.at[k, slot], g_send.at[k, n], g_recv.at[k, n], (sec, target)
        )

    def relay(k):
        for d in range(1, chips):
            g_copy(k, 1, d, behind(d), ahead(d)).wait_recv()
            g_copy(k, 2, d, behind(d), pair).start()

    def accumulate(k, last=False):
        g_copy(k, 0, 0, pair, pair).wait_recv()
        for d in range(1, chips):
            g_copy(k, 2, d, behind(d, False), pair).wait_recv()
        lhs = normed_all[k].reshape(shards * rows, blk)
        for b in range(4):
            cols = slice(b * (width // 4), (b + 1) * (width // 4))
            rhs = grads[k, :, :, cols].reshape(shards * rows, width // 4)
            term = lax.dot_general(lhs, rhs, TN, preferred_element_type=f32)
            if last:
                dproj[:, cols] = (total[:, cols] + term).astype(bf16)
            else:
                total[:, cols] += term

    lag = jnp.where(sec == 0, 1, jnp.clip(2 + 3 * (sec - (top - 4)), 4, chunks - 1))

    def columns_here():
        for d in range(1, shards):
            n_copy(d, me, lax.rem(me + shards - d, shards)).wait_recv()

    def section_back(k, back_of, grad_of):
        inv = inv_rms[k]
        dots = jnp.zeros((rows, 1), f32)
        for b in range(shards):
            cols = slice(b * blk, (b + 1) * blk)
            back = back_of(b)
            back_s[:, cols] = back
            prod = back * (acts[k, :, cols].astype(f32) * inv)
            gain_acc[:, cols] += jnp.sum(prod, 0, keepdims=True)
            dots = dots + jnp.sum(prod * gain[:, cols], -1, keepdims=True)
        mean = dots / width
        for b in range(shards):
            cols = slice(b * blk, (b + 1) * blk)
            x_hat = acts[k, :, cols].astype(f32) * inv
            through = inv * (back_s[:, cols] * gain[:, cols] - x_hat * mean)
            din[k, :, cols] = (grad_of(cols) + through).astype(bf16)

        @pl.when(sec > 0)
        def _():
            c_copy(k).start()

    def top_step(k, carry):
        def pick(value):
            return lax.dot_general(pool[k], value, TN, preferred_element_type=f32)

        section_back(
            k,
            lambda b: pick(normed_all[5, b, 0:every]),
            lambda cols: pick(grads[0, me, 0:every, cols]),
        )
        return carry

    def step(k, carry):
        c_copy(k).wait_recv()
        g_copy(k, 0, 0, me, pair).start()
        for d in range(1, chips):
            g_copy(k, 1, d, me, ahead(d)).start()
        section_back(
            k,
            lambda b: jnp.dot(grads[k, me], weight[b], preferred_element_type=f32),
            lambda cols: grads[k, me, :, cols].astype(f32),
        )

        @pl.when(k >= lag)
        def _():
            relay(k - lag)

        @pl.when(k == lag + 1)
        def _():
            columns_here()

        @pl.when(k >= lag + 1)
        def _():
            accumulate(k - lag - 1)

        return carry

    @pl.when(is_top)
    def _():
        lax.fori_loop(0, chunks, top_step, 0)

    @pl.when(sec < top)
    def _():
        lax.fori_loop(0, chunks, step, 0)

    def d_copy(d, slot):
        return remote(
            gain_acc, gain_all.at[slot], d_send.at[d - 1], d_recv.at[d - 1],
            (sec, lax.rem(me + d, shards)),
        )

    for d in range(1, shards):
        d_copy(d, me).start()

    @pl.when(is_top)
    def _():
        every_grad = flat(grads[0, :, 0:every])
        for n in (2, 3):
            sums = flat(normed_all[n, :, 0:every])
            for b in range(4):
                cols = slice(b * quarter, (b + 1) * quarter)
                total[:, cols] += lax.dot_general(
                    sums, every_grad[:, cols], TN, preferred_element_type=f32
                )
        dproj[...] = total[...].astype(bf16)

    def catch_up(k, carry):
        accumulate(k - 1)
        relay(k)
        return carry

    @pl.when(sec < top)
    def _():
        @pl.when(lag + 1 >= chunks)
        def _():
            columns_here()

        lax.fori_loop(chunks - lag, chunks, catch_up, 0)
        accumulate(chunks - 1, last=True)

    gain_all[me] = gain_acc[...]
    for d in range(1, shards):
        d_copy(d, lax.rem(me + shards - d, shards)).wait_recv()
    dgain[...] = jnp.sum(gain_all[...], 0)

    for d in range(1, shards):
        d_copy(d, me).wait_send()

    @pl.when(is_top)
    def _():
        for d in range(1, shards):
            sums_out(d).wait_send()
            counts_out(d).wait_send()
            parts_out(d).wait_send()
            logits_out(d).wait_send()
            backs_out(d).wait_send()

    @pl.when(sec < top)
    def _():
        for p in range(PIECES):
            w_copy(p, 0, 0, me, pair, own=True).wait_send()
            for d in range(1, chips):
                w_copy(p, 2, d, behind(d), pair).wait_send()
        for p in direct:
            for d in range(1, chips):
                w_copy(p, 1, d, me, ahead(d), own=True).wait_send()

        @pl.when(lone)
        def _():
            for p in lent:
                for d in range(1, chips):
                    w_copy(p, 1, d, me, ahead(d), own=True).wait_send()

        for d in range(1, shards):
            n_copy(d, lax.rem(me + d, shards), me).wait_send()

    if lending:
        @pl.when(borrows)
        def _():
            for i in range(LENT):
                v_copy(0, i).wait_send()

        @pl.when(lends)
        def _():
            for i in range(LENT):
                v_copy(1, i).wait_send()
                v_copy(2, i).wait_send()

    def sent(k, carry):
        @pl.when(sec > 0)
        def _():
            c_copy(k).wait_send()

        @pl.when(sec < top)
        def _():
            g_copy(k, 0, 0, me, pair).wait_send()
            for d in range(1, chips):
                g_copy(k, 1, d, me, ahead(d)).wait_send()
                g_copy(k, 2, d, behind(d), pair).wait_send()

        return carry

    lax.fori_loop(0, chunks, sent, 0)


def per_device(sections, shards, acts, gains, proj, head, segs, labels):
    tokens, width = acts.shape[1:]
    batches, rows = segs.shape
    cands = labels.shape[1]
    classes = head.shape[1]
    blk = proj.shape[1]
    chunks = tokens // CHUNK
    chips = shards // 2
    every = batches * cands
    vmem = pl.BlockSpec(memory_space=pltpu.VMEM)
    hbm = pl.BlockSpec(memory_space=pl.ANY)
    dma = pltpu.SemaphoreType.DMA
    din, dproj, dgain = pl.pallas_call(
        functools.partial(kernel, sections, shards, chunks),
        out_shape=(
            jax.ShapeDtypeStruct((chunks, CHUNK, width), bf16),
            jax.ShapeDtypeStruct((blk, width), bf16),
            jax.ShapeDtypeStruct((1, width), f32),
        ),
        in_specs=[hbm, vmem, hbm, hbm, vmem, vmem],
        out_specs=(vmem, vmem, vmem),
        scratch_shapes=[
            pltpu.VMEM((chunks, CHUNK, width), bf16),
            pltpu.VMEM((width, classes), bf16),
            pltpu.VMEM((shards, width, blk), bf16),
            pltpu.VMEM((chunks, shards, CHUNK, width), bf16),
            pltpu.VMEM((shards, chunks, CHUNK, blk), bf16),
            pltpu.VMEM((chunks, shards, CHUNK, blk), bf16),
            pltpu.VMEM((chunks, CHUNK, 1), f32),
            pltpu.VMEM((CHUNK, width), f32),
            pltpu.VMEM((blk, width), f32),
            pltpu.VMEM((1, width), f32),
            pltpu.VMEM((shards, 1, width), f32),
            pltpu.VMEM((chunks, every, CHUNK), bf16),
            pltpu.VMEM((shards, every, classes), f32),
            pltpu.VMEM((shards, every, classes), f32),
            pltpu.VMEM((LENT, width // PIECES if chips == 2 else 16, blk), bf16),
            pltpu.VMEM((LENT, width // PIECES if chips == 2 else 16, blk), bf16),
            dma((3,)),
            dma((PIECES, 2 * chips - 1)),
            dma((PIECES, 2 * chips - 1)),
            dma((shards - 1,)),
            dma((shards - 1,)),
            dma((chunks,)),
            dma((chunks,)),
            dma((chunks, 2 * chips - 1)),
            dma((chunks, 2 * chips - 1)),
            dma((shards - 1,)),
            dma((shards - 1,)),
            dma((5, shards - 1)),
            dma((5, shards - 1)),
            dma((3, LENT)),
            dma((3, LENT)),
        ],
        compiler_params=pltpu.CompilerParams(
            collective_id=0, has_side_effects=True, vmem_limit_bytes=127 * 512 * 1024
        ),
        cost_estimate=pl.CostEstimate(
            flops=4 * tokens * width * width, bytes_accessed=16 * width * width, transcendentals=0
        ),
    )(
        acts[0].reshape(chunks, CHUNK, width),
        gains,
        proj[0].T,
        head,
        segs,
        labels,
    )
    return din.reshape(1, tokens, width), dproj[None], dgain


def solution(mesh):
    return jax.shard_map(
        functools.partial(per_device, mesh.shape["section"], mesh.shape["fsdp"]),
        mesh=mesh,
        in_specs=(
            P("section", "fsdp", None),
            P("section", None),
            P("section", "fsdp", None),
            P(),
            P("fsdp", None),
            P("fsdp", None),
        ),
        out_specs=(P("section", "fsdp", None), P("section", "fsdp", None), P("section", None)),
        check_vma=False,
    )
```
